32 devices in a mesh: tensor: 4 (over z), expert: 8 (over y, x, core).
Axes of the slice: x: 2, y: 2, z: 4, core: 2. Of those that a mesh axis runs over, the one named last changes fastest.
Arguments:
- tokens: bfloat16 [1024, 7168], P('expert', 'tensor'), may hold values from -6 to 6
- route_ids: int32 [1024, 2], P('expert'), may hold values from 0 to 7, all different within a row; in each aligned block of 128 rows (0 to 127, 128 to 255, ...) at most 64 rows name the same one
- route_weights: float32 [1024, 2], P('expert'), may hold values from 0.1 to 1
- cotangent: bfloat16 [1024, 7168], P('expert', 'tensor'), may hold values from -6 to 6
- w_gate: bfloat16 [8, 7168, 1024], P('expert', None, 'tensor'), may hold values from -0.0625 to 0.0625
- w_up: bfloat16 [8, 7168, 1024], P('expert', None, 'tensor'), may hold values from -0.0625 to 0.0625
- w_down: bfloat16 [8, 1024, 7168], P('expert', 'tensor'), may hold values from -0.1875 to 0.1875
Outputs:
- mixed: bfloat16 [1024, 7168], P('expert', 'tensor')
- grad_tokens: bfloat16 [1024, 7168], P('expert', 'tensor')
- grad_route: float32 [1024, 2], P('expert')
- grad_gate: bfloat16 [8, 7168, 1024], P('expert', None, 'tensor')
- grad_up: bfloat16 [8, 7168, 1024], P('expert', None, 'tensor')
- grad_down: bfloat16 [8, 1024, 7168], P('expert', 'tensor')
The draws below stay inside these ranges and needn't reach their ends.
Inputs may be any that keep to these rules, and one draw needn't show every extreme that they name: `route_ids`: each row names 2 different experts. In each aligned block of 128 rows (the rows of one device) no expert is named by more than 64 rows, and in some block one expert is named by exactly 64 rows.
All inputs are finite; a program needn't handle non-finite values.
Results may differ from the reference program's by a relative error of at most 0.015.
Values may be sent and summed in bfloat16 or wider, within the bound.
No kernel may reach another device: no remote copies, remote signals or barrier semaphores. Data moves between devices by JAX's collectives and lax.ppermute only.
A program may use at most 128 MiB of HBM per device.

```python
import math
import jax
import jax.numpy as jnp
import numpy as np
from jax import lax

D = 7168
FF = 1024
TOPK = 2
TOK_DEV = 128
EXPERTS = 8
CAP = 64
TOKENS = 1024
N_TENSOR = 4
N_EXPERT = 8


def levels(stream_key, dims, cuts, low, top_value):
    loudness, own = 1.0, jax.random.fold_in(stream_key, 6)
    for dim, blocks in cuts:
        steps = jnp.exp(jax.random.uniform(jax.random.fold_in(own, dim), (blocks,), jnp.float32, low / len(cuts), top_value / len(cuts)))
        loudness = loudness * jnp.repeat(steps, dims[dim] // blocks).reshape([-1 if axis == dim else 1 for axis in range(len(dims))])
    return loudness


def deal_out(own_key, own, number, rows, number_of, top, bound, skew):
    order = jax.random.permutation(own_key, number_of)
    heavy_load, usual = portions_of(number_of, rows * top, bound, skew, True), portions_of(number_of, rows * top, bound, skew, False)
    places = jnp.arange(number_of)

    def named(lengths, rotation):
        used = int((lengths > 0).sum())
        fixed = max(1, used // 4)
        passed = fixed + (places - fixed + rotation * (used - fixed)) % max(1, number_of - fixed)
        return jnp.zeros((number_of,), jnp.int32).at[order[jnp.where(places < fixed, places, passed)]].set(jnp.asarray(lengths, jnp.int32))

    lengths = jnp.where(number % 4 == 0, named(heavy_load, number // 4), named(usual, number - number // 4 - 1))
    mixed = jax.random.permutation(jax.random.fold_in(own, 3), number_of)
    source_of, receiver = mixed[0:number_of // 2 * 2:2], mixed[1:number_of // 2 * 2:2]
    slack = jnp.minimum(lengths[source_of] - 1, bound - lengths[receiver]) // 2
    slack = jnp.where((source_of == order[0]) | (receiver == order[0]) | (lengths[receiver] == 0), 0, jnp.maximum(slack, 0))
    passed = jax.random.randint(jax.random.fold_in(own, 4), (number_of // 2,), 0, 1 << 20) % (slack + 1)
    lengths = lengths.at[source_of].add(-passed).at[receiver].add(passed)
    items = jnp.searchsorted(jnp.cumsum(lengths), jnp.arange(rows * top), side="right").astype(jnp.int32)
    grid = items.reshape(top, rows).T
    grid = grid[jax.random.permutation(jax.random.fold_in(own, 1), rows)]
    rotation = jax.random.randint(jax.random.fold_in(own, 2), (rows, 1), 0, top)
    return jnp.take_along_axis(grid, (jnp.arange(top)[None, :] + rotation) % top, axis=1)


def portions_of(number_of, total, reach, skew, full):
    loads = [(1 << 20) // math.isqrt(standing ** skew) + 1 for standing in range(1, number_of + 1)]
    largest = reach if full else min(reach, max(-(-total // number_of), total * loads[0] // sum(loads)))
    least = 1 if total - largest >= number_of - 1 else 0
    holding, surplus = [largest] + [least] * (number_of - 1), total - largest - least * (number_of - 1)
    while surplus > 0:
        movable = [i for i in range(1, number_of) if holding[i] < largest] or [i for i in range(1, number_of) if holding[i] < reach]
        whole, remaining = sum([loads[i] for i in movable]), surplus
        for i in movable:
            extra = min(reach - holding[i], max(1, remaining * loads[i] // whole), surplus)
            holding[i] = holding[i] + extra
            surplus = surplus - extra
    return np.array(holding)


def bell_draw(own_key, extent, width, reach, cuts=(), kind=jnp.bfloat16):
    loudness = levels(own_key, extent, cuts, -0.22, 0.18) if cuts else 1.0
    result = jax.random.normal(own_key, extent, jnp.float32) * width * loudness
    return jnp.minimum(jnp.maximum(result, -reach), reach).astype(kind)


def setup_inputs(seed: int = 0) -> dict:
    key_list = jax.random.split(jax.random.key(seed), 8)
    tokens = bell_draw(key_list[0], (TOKENS, D), 1.0, 6.0, ((0, 8), (1, 4)))
    route_ids_keys = jax.random.split(jax.random.fold_in(key_list[1], 1), TOKENS // TOK_DEV)
    route_ids_turns = jax.random.permutation(jax.random.fold_in(key_list[1], 3), TOKENS // TOK_DEV)
    route_ids = jax.vmap(lambda own, number: deal_out(jax.random.fold_in(key_list[1], 2), own, number, TOK_DEV, EXPERTS, TOPK, CAP, 2))(route_ids_keys, route_ids_turns).reshape((TOKENS, TOPK))
    route_weights = jnp.clip(jnp.exp(math.log(1.0) - 2.3025851 * jax.random.uniform(key_list[2], (TOKENS, TOPK), jnp.float32) ** levels(key_list[2], (TOKENS, TOPK), ((0, 8),), -0.2, 0.2)), 0.1, 1.0)
    cotangent = bell_draw(key_list[3], (TOKENS, D), 1.0, 6.0, ((0, 8), (1, 4)))
    w_gate = bell_draw(key_list[4], (EXPERTS, D, FF), D ** -0.5, 0.0625, ((0, 8), (2, 4)))
    w_up = bell_draw(key_list[5], (EXPERTS, D, FF), D ** -0.5, 0.0625, ((0, 8), (2, 4)))
    w_down = bell_draw(key_list[6], (EXPERTS, FF, D), FF ** -0.5, 0.1875, ((0, 8), (1, 4)))
    return {"tokens": tokens, "route_ids": route_ids, "route_weights": route_weights, "cotangent": cotangent, "w_gate": w_gate, "w_up": w_up, "w_down": w_down}


def slot_positions(route_ids):
    flat_ids = route_ids.reshape(N_EXPERT, TOK_DEV * TOPK)
    labels = jnp.arange(EXPERTS, dtype=jnp.int32)
    onehot = (flat_ids[:, :, None] == labels[None, None, :]).astype(jnp.int32)
    before = jnp.cumsum(onehot, axis=1) - onehot
    slot_index = jnp.sum(before * onehot, axis=2)
    source_block = jnp.arange(N_EXPERT, dtype=jnp.int32)[:, None]
    target = (flat_ids * N_EXPERT + source_block) * CAP + slot_index
    return target.reshape(TOKENS * TOPK).astype(jnp.int32)


def per_block_total(parts):
    rounded = lax.optimization_barrier(parts.astype(jnp.bfloat16))
    return jnp.sum(rounded.astype(jnp.float32), axis=0)


def column_split(matrix):
    block_width = FF // N_TENSOR
    return matrix.astype(jnp.float32).reshape(matrix.shape[0], N_TENSOR, block_width).transpose(1, 0, 2)


def expert_pass(operands):
    rows, cot_rows, gate_matrix, up_matrix, down_weight = operands
    block_width = FF // N_TENSOR
    row_pairs = (((1,), (1,)), ((), ()))
    col_pairs = (((0,), (0,)), ((), ()))
    gate_proj = jnp.dot(rows, gate_matrix, preferred_element_type=jnp.float32)
    up_proj = jnp.dot(rows, up_matrix, preferred_element_type=jnp.float32)
    hidden_state = (jax.nn.silu(gate_proj) * up_proj).astype(jnp.bfloat16)
    down_block_list = down_weight.astype(jnp.float32).reshape(N_TENSOR, block_width, D)
    expert_output = per_block_total(jnp.einsum("zej,zjq->zeq", column_split(hidden_state), down_block_list)).astype(jnp.bfloat16)
    d_hidden = lax.dot_general(cot_rows, down_weight, row_pairs, preferred_element_type=jnp.float32)
    grad_down = lax.dot_general(hidden_state, cot_rows, col_pairs, preferred_element_type=jnp.float32).astype(jnp.bfloat16)
    sigmoid_gate = jax.nn.sigmoid(gate_proj)
    gate_gradient = (d_hidden * up_proj * sigmoid_gate * (1.0 + gate_proj * (1.0 - sigmoid_gate))).astype(jnp.bfloat16)
    up_gradient = (d_hidden * jax.nn.silu(gate_proj)).astype(jnp.bfloat16)
    grad_gate = lax.dot_general(rows, gate_gradient, col_pairs, preferred_element_type=jnp.float32).astype(jnp.bfloat16)
    grad_up = lax.dot_general(rows, up_gradient, col_pairs, preferred_element_type=jnp.float32).astype(jnp.bfloat16)
    backward_pieces = jnp.einsum("snu,syu->sny", column_split(gate_gradient), column_split(gate_matrix))
    backward_pieces = backward_pieces + jnp.einsum("snu,syu->sny", column_split(up_gradient), column_split(up_matrix))
    input_rows = per_block_total(backward_pieces).astype(jnp.bfloat16)
    return expert_output, input_rows, grad_gate, grad_up, grad_down


def reference(tokens, route_ids, route_weights, cotangent, w_gate, w_up, w_down):
    target = slot_positions(route_ids)
    pair_rows = jnp.repeat(tokens, TOPK, axis=0)
    weight_flat = route_weights.reshape(TOKENS * TOPK)
    cot_pairs = (weight_flat[:, None] * jnp.repeat(cotangent, TOPK, axis=0).astype(jnp.float32)).astype(jnp.bfloat16)
    buffer_rows = EXPERTS * N_EXPERT * CAP
    routed = jnp.zeros((buffer_rows, D), jnp.bfloat16).at[target].set(pair_rows)
    routed_cot = jnp.zeros((buffer_rows, D), jnp.bfloat16).at[target].set(cot_pairs)
    stacked_shape = (EXPERTS, N_EXPERT * CAP, D)
    expert_output, input_rows, grad_gate, grad_up, grad_down = lax.map(
        expert_pass, (routed.reshape(stacked_shape), routed_cot.reshape(stacked_shape), w_gate, w_up, w_down))
    chosen = expert_output.reshape(buffer_rows, D)[target].astype(jnp.float32).reshape(TOKENS, TOPK, D)
    mixed = jnp.sum(route_weights[:, :, None] * chosen, axis=1).astype(jnp.bfloat16)
    grad_route = jnp.sum(cotangent.astype(jnp.float32)[:, None, :] * chosen, axis=2)
    chosen_grads = input_rows.reshape(buffer_rows, D)[target].astype(jnp.float32).reshape(TOKENS, TOPK, D)
    grad_tokens = jnp.sum(route_weights[:, :, None] * chosen_grads, axis=1).astype(jnp.bfloat16)
    return (mixed, grad_tokens, grad_route, grad_gate, grad_up, grad_down)
```

```python
import jax
import jax.numpy as jnp
from jax import lax
from jax.sharding import PartitionSpec as P

TOPK = 2


ROW_PAIRS = (((1,), (1,)), ((), ()))
COLUMN_PAIRS = (((0,), (0,)), ((), ()))


def slot_tables(route_ids, experts, capacity):
    pair_count = route_ids.shape[0] * route_ids.shape[1]
    flat_ids = route_ids.reshape(pair_count)
    labels = jnp.arange(experts, dtype=jnp.int32)
    onehot = (flat_ids[:, None] == labels[None, :]).astype(jnp.int32)
    before = jnp.cumsum(onehot, axis=0) - onehot
    slot_index = jnp.sum(before * onehot, axis=1)
    target = flat_ids * capacity + slot_index
    source = (
        jnp.full((experts * capacity,), pair_count, jnp.int32)
        .at[target]
        .set(jnp.arange(pair_count, dtype=jnp.int32))
    )
    return (target, source)


def fill_slots(token_part, cot_part, weight_flat, source):
    row_of = source // TOPK
    zero_row = jnp.zeros((1, token_part.shape[1]), jnp.bfloat16)
    padded_tokens = jnp.concatenate([token_part, zero_row], axis=0)
    padded_cot = jnp.concatenate([cot_part, zero_row], axis=0)
    padded_weight = jnp.concatenate([weight_flat, jnp.zeros((1,), jnp.float32)], axis=0)
    token_slots = padded_tokens[row_of]
    cot_slots = (padded_weight[source][:, None] * padded_cot[row_of].astype(jnp.float32)).astype(
        jnp.bfloat16
    )
    return (token_slots, cot_slots)


def slot_plan(tokens, route_ids, route_weights, cotangent, w_gate, w_up, w_down):
    experts = lax.axis_size("expert")
    tok_rows, slice_width = tokens.shape
    capacity = 4 * tok_rows // experts
    gate_matrix = w_gate[0]
    up_matrix = w_up[0]
    down_weight = w_down[0]
    target, source = slot_tables(route_ids, experts, capacity)
    weight_flat = route_weights.reshape(tok_rows * TOPK)
    full_tokens, full_cot = (
        lax.all_gather(tokens, "tensor", axis=1, tiled=True),
        lax.all_gather(cotangent, "tensor", axis=1, tiled=True),
    )
    model_width = full_tokens.shape[1]
    token_slots, cot_slots = fill_slots(full_tokens, full_cot, weight_flat, source)
    routed, routed_cot = (
        lax.all_to_all(
            token_slots.reshape(experts, capacity, model_width),
            "expert",
            split_axis=0,
            concat_axis=0,
            tiled=True,
        ),
        lax.all_to_all(
            cot_slots.reshape(experts, capacity, model_width),
            "expert",
            split_axis=0,
            concat_axis=0,
            tiled=True,
        ),
    )
    routed = routed.reshape(experts * capacity, model_width)
    routed_cot = routed_cot.reshape(experts * capacity, model_width)
    gate_proj = jnp.dot(routed, gate_matrix, preferred_element_type=jnp.float32)
    up_proj = jnp.dot(routed, up_matrix, preferred_element_type=jnp.float32)
    hidden_state = (jax.nn.silu(gate_proj) * up_proj).astype(jnp.bfloat16)
    down_part = jnp.dot(hidden_state, down_weight, preferred_element_type=jnp.float32)
    expert_sum = lax.psum_scatter(
        down_part.astype(jnp.bfloat16), "tensor", scatter_dimension=1, tiled=True
    )
    expert_output = expert_sum.reshape(experts, capacity, slice_width)
    returned = lax.all_to_all(
        expert_output, "expert", split_axis=0, concat_axis=0, tiled=True
    ).reshape(experts * capacity, slice_width)
    chosen = returned[target].astype(jnp.float32).reshape(tok_rows, TOPK, slice_width)
    mixed = jnp.sum(route_weights[:, :, None] * chosen, axis=1).astype(jnp.bfloat16)
    route_part = jnp.sum(cotangent.astype(jnp.float32)[:, None, :] * chosen, axis=2)
    grad_route = lax.psum(route_part, "tensor")
    d_hidden = lax.dot_general(
        routed_cot, down_weight, ROW_PAIRS, preferred_element_type=jnp.float32
    )
    grad_down = lax.dot_general(
        hidden_state, routed_cot, COLUMN_PAIRS, preferred_element_type=jnp.float32
    ).astype(jnp.bfloat16)
    sigmoid_gate = jax.nn.sigmoid(gate_proj)
    gate_gradient = (
        d_hidden * up_proj * sigmoid_gate * (1.0 + gate_proj * (1.0 - sigmoid_gate))
    ).astype(jnp.bfloat16)
    up_gradient = (d_hidden * jax.nn.silu(gate_proj)).astype(jnp.bfloat16)
    grad_gate = lax.dot_general(
        routed, gate_gradient, COLUMN_PAIRS, preferred_element_type=jnp.float32
    ).astype(jnp.bfloat16)
    grad_up = lax.dot_general(
        routed, up_gradient, COLUMN_PAIRS, preferred_element_type=jnp.float32
    ).astype(jnp.bfloat16)
    back_part = lax.dot_general(
        gate_gradient, gate_matrix, ROW_PAIRS, preferred_element_type=jnp.float32
    )
    back_part = back_part + lax.dot_general(
        up_gradient, up_matrix, ROW_PAIRS, preferred_element_type=jnp.float32
    )
    input_sum = lax.psum_scatter(
        back_part.astype(jnp.bfloat16), "tensor", scatter_dimension=1, tiled=True
    )
    input_rows = input_sum.reshape(experts, capacity, slice_width)
    returned_grads = lax.all_to_all(
        input_rows, "expert", split_axis=0, concat_axis=0, tiled=True
    ).reshape(experts * capacity, slice_width)
    chosen_grads = returned_grads[target].astype(jnp.float32).reshape(tok_rows, TOPK, slice_width)
    grad_tokens = jnp.sum(route_weights[:, :, None] * chosen_grads, axis=1).astype(jnp.bfloat16)
    return (mixed, grad_tokens, grad_route, grad_gate[None], grad_up[None], grad_down[None])


def xor_pairs(bit):
    return [(i, i ^ bit) for i in range(lax.axis_size("expert"))]


def over_core(value):
    return lax.ppermute(value, "expert", xor_pairs(1))


def over_x(value):
    return lax.ppermute(value, "expert", xor_pairs(2))


def over_y(value):
    return lax.ppermute(value, "expert", xor_pairs(4))


def over_z(value):
    count = lax.axis_size("tensor")
    return lax.ppermute(value, "tensor", [(i, (i + 1) % count) for i in range(count)])


def gather_rows(part, count):
    pieces = []
    own = part
    for step in range(count):
        side, front = over_x(own), over_y(own)
        far = over_y(side) if step % 2 == 0 else over_x(front)
        pieces.append(jnp.concatenate([own, side, front, far], axis=0))
        if step < count - 1:
            own = over_z(own)
    return pieces


def scatter_rows(product, rows, count, place):
    def rounded(blocks, part):
        return product(blocks, part).astype(jnp.bfloat16)

    total = None
    for step in range(count):
        part = lax.rem(place + 2 * count - 1 - step, count)
        if step % 2 == 0:
            came = over_x(rounded((1, 3), part))
            kept = (product((0, 2), part) + came.astype(jnp.float32))
            last = over_y(kept[rows:].astype(jnp.bfloat16))
        else:
            came = over_y(rounded((2, 3), part))
            kept = (product((0, 1), part) + came.astype(jnp.float32))
            last = over_x(kept[rows:].astype(jnp.bfloat16))
        here = kept[:rows] + last.astype(jnp.float32)
        if total is not None:
            here = here + total.astype(jnp.float32)
        here = here.astype(jnp.bfloat16)
        total = over_z(here) if step < count - 1 else here
    return total


def dot(a, b, dims=(((1,), (0,)), ((), ()))):
    return lax.dot_general(a, b, dims, preferred_element_type=jnp.float32)


def chip_plan(tokens, route_ids, route_weights, cotangent, w_gate, w_up, w_down):
    count = lax.axis_size("tensor")
    experts = lax.axis_size("expert")
    place, me = lax.axis_index("tensor"), lax.axis_index("expert")
    rows, width = tokens.shape
    units = w_gate.shape[2]

    wide = jnp.concatenate([w_gate[0], w_up[0]], axis=1)
    wide = jnp.concatenate([wide, over_core(wide)], axis=1)
    tall = jnp.concatenate([w_down[0], over_core(w_down[0])], axis=0)

    labels = jnp.arange(experts, dtype=jnp.int32)
    named = route_ids[:, :, None] == labels[None, None, :]
    shares = jnp.sum(jnp.where(named, route_weights[:, :, None], 0.0), axis=1)
    shares_x, shares_y = over_x(shares), over_y(shares)
    shares = jnp.concatenate([shares, shares_x, shares_y, over_y(shares_x)], axis=0)
    share = [
        lax.dynamic_slice_in_dim(shares, me, 1, 1),
        lax.dynamic_slice_in_dim(shares, me ^ 1, 1, 1),
    ]

    def part_of(step):
        return lax.rem(place + count - step, count)

    def wide_part(part):
        return lax.dynamic_slice_in_dim(wide, part * width, width, 0)

    def tall_part(part):
        return lax.dynamic_slice_in_dim(tall, part * width, width, 1)

    token_parts = gather_rows(tokens, count)
    cot_parts = gather_rows(cotangent, count)

    both = sum(dot(token_parts[k], wide_part(part_of(k))) for k in range(count))
    d_both = sum(dot(cot_parts[k], tall_part(part_of(k)), ROW_PAIRS) for k in range(count))
    weighted, to_weights, to_tokens, inner = [], [], [], []
    for i in range(2):
        gate = both[:, (2 * i) * units : (2 * i + 1) * units]
        up = both[:, (2 * i + 1) * units : (2 * i + 2) * units]
        d_plain = d_both[:, i * units : (i + 1) * units]
        sigmoid_gate = jax.nn.sigmoid(gate)
        silu_gate = gate * sigmoid_gate
        hidden = silu_gate * up
        weighted.append((share[i] * hidden).astype(jnp.bfloat16))
        inner.append(jnp.sum(hidden * d_plain, axis=1, keepdims=True))
        d_hidden = share[i] * d_plain
        d_gate = d_hidden * up * sigmoid_gate * (1.0 + gate * (1.0 - sigmoid_gate))
        d_up = d_hidden * silu_gate
        to_weights += [d_gate.astype(jnp.bfloat16), d_up.astype(jnp.bfloat16)]
        to_tokens += [(share[i] * d_gate).astype(jnp.bfloat16), (share[i] * d_up).astype(jnp.bfloat16)]
    weighted = jnp.concatenate(weighted, axis=1)
    to_tokens = jnp.concatenate(to_tokens, axis=1)

    def blocks_of(matrix, blocks):
        return jnp.concatenate([matrix[b * rows : (b + 1) * rows] for b in blocks], axis=0)

    mixed = scatter_rows(
        lambda blocks, part: dot(blocks_of(weighted, blocks), tall_part(part)), rows, count, place
    )
    grad_tokens = scatter_rows(
        lambda blocks, part: dot(blocks_of(to_tokens, blocks), wide_part(part), ROW_PAIRS),
        rows,
        count,
        place,
    )

    inner = jnp.concatenate(inner, axis=1)
    turns = [inner]
    for _ in range(count - 1):
        turns.append(over_z(turns[-1]))
    turns = jnp.stack(turns)
    inner = sum(lax.dynamic_index_in_dim(turns, part_of(k), 0, False) for k in range(count))
    blocks = [inner[b * rows : (b + 1) * rows] for b in range(4)]
    inner = [blocks[0], over_x(blocks[1]), over_y(blocks[2]), over_y(over_x(blocks[3]))]
    grad_route = 0.0
    for q in range(4):
        for i in range(2):
            grad_route += jnp.where(route_ids == me ^ (2 * q) ^ i, inner[q][:, i : i + 1], 0.0)

    own_cols = jnp.concatenate(to_weights[:2], axis=1)
    other_cols = jnp.concatenate(to_weights[2:], axis=1)
    grad_wide = [dot(token_parts[k], other_cols, COLUMN_PAIRS).astype(jnp.bfloat16) for k in range(count)]
    grad_tall = [
        dot(weighted[:, units:], cot_parts[k], COLUMN_PAIRS).astype(jnp.bfloat16) for k in range(count)
    ]
    grad_wide = [over_core(g) for g in grad_wide]
    grad_tall = [over_core(g) for g in grad_tall]
    grad_gate = jnp.zeros(w_gate.shape[1:], jnp.bfloat16)
    grad_up = jnp.zeros(w_up.shape[1:], jnp.bfloat16)
    grad_down = jnp.zeros(w_down.shape[1:], jnp.bfloat16)
    for k in range(count):
        part = part_of(k)
        both_grads = dot(token_parts[k], own_cols, COLUMN_PAIRS) + grad_wide[k].astype(jnp.float32)
        both_grads = both_grads.astype(jnp.bfloat16)
        down = dot(weighted[:, :units], cot_parts[k], COLUMN_PAIRS) + grad_tall[k].astype(jnp.float32)
        grad_gate = lax.dynamic_update_slice_in_dim(grad_gate, both_grads[:, :units], part * width, 0)
        grad_up = lax.dynamic_update_slice_in_dim(grad_up, both_grads[:, units:], part * width, 0)
        grad_down = lax.dynamic_update_slice_in_dim(
            grad_down, down.astype(jnp.bfloat16), part * width, 1
        )
    return (mixed, grad_tokens, grad_route, grad_gate[None], grad_up[None], grad_down[None])


def local(tokens, route_ids, route_weights, cotangent, w_gate, w_up, w_down):
    experts = lax.axis_size("expert")
    capacity = 4 * tokens.shape[0] // experts
    plan = chip_plan if 2 * capacity >= tokens.shape[0] and experts == 8 else slot_plan
    return plan(tokens, route_ids, route_weights, cotangent, w_gate, w_up, w_down)


def solution(mesh):
    placed = (
        P("expert", "tensor"),
        P("expert", None),
        P("expert", None),
        P("expert", "tensor"),
        P("expert", None, "tensor"),
        P("expert", None, "tensor"),
        P("expert", "tensor", None),
    )
    return jax.shard_map(
        local,
        mesh=mesh,
        in_specs=placed,
        out_specs=(
            P("expert", "tensor"),
            P("expert", "tensor"),
            P("expert", None),
            P("expert", None, "tensor"),
            P("expert", None, "tensor"),
            P("expert", "tensor", None),
        ),
        check_vma=False,
    )
```

```python
import jax
import jax.numpy as jnp
from jax import lax
from jax.experimental import pallas as pl
from jax.experimental.pallas import tpu as pltpu
from jax.sharding import PartitionSpec as P

TOPK = 2


ROW_PAIRS = (((1,), (1,)), ((), ()))
COLUMN_PAIRS = (((0,), (0,)), ((), ()))


def slot_tables(route_ids, experts, capacity):
    pair_count = route_ids.shape[0] * route_ids.shape[1]
    flat_ids = route_ids.reshape(pair_count)
    labels = jnp.arange(experts, dtype=jnp.int32)
    onehot = (flat_ids[:, None] == labels[None, :]).astype(jnp.int32)
    before = jnp.cumsum(onehot, axis=0) - onehot
    slot_index = jnp.sum(before * onehot, axis=1)
    target = flat_ids * capacity + slot_index
    source = (
        jnp.full((experts * capacity,), pair_count, jnp.int32)
        .at[target]
        .set(jnp.arange(pair_count, dtype=jnp.int32))
    )
    return (target, source)


def fill_slots(token_part, cot_part, weight_flat, source):
    row_of = source // TOPK
    zero_row = jnp.zeros((1, token_part.shape[1]), jnp.bfloat16)
    padded_tokens = jnp.concatenate([token_part, zero_row], axis=0)
    padded_cot = jnp.concatenate([cot_part, zero_row], axis=0)
    padded_weight = jnp.concatenate([weight_flat, jnp.zeros((1,), jnp.float32)], axis=0)
    token_slots = padded_tokens[row_of]
    cot_slots = (padded_weight[source][:, None] * padded_cot[row_of].astype(jnp.float32)).astype(
        jnp.bfloat16
    )
    return (token_slots, cot_slots)


def slot_plan(tokens, route_ids, route_weights, cotangent, w_gate, w_up, w_down):
    experts = lax.axis_size("expert")
    tok_rows, slice_width = tokens.shape
    capacity = 4 * tok_rows // experts
    gate_matrix = w_gate[0]
    up_matrix = w_up[0]
    down_weight = w_down[0]
    target, source = slot_tables(route_ids, experts, capacity)
    weight_flat = route_weights.reshape(tok_rows * TOPK)
    full_tokens, full_cot = (
        lax.all_gather(tokens, "tensor", axis=1, tiled=True),
        lax.all_gather(cotangent, "tensor", axis=1, tiled=True),
    )
    model_width = full_tokens.shape[1]
    token_slots, cot_slots = fill_slots(full_tokens, full_cot, weight_flat, source)
    routed, routed_cot = (
        lax.all_to_all(
            token_slots.reshape(experts, capacity, model_width),
            "expert",
            split_axis=0,
            concat_axis=0,
            tiled=True,
        ),
        lax.all_to_all(
            cot_slots.reshape(experts, capacity, model_width),
            "expert",
            split_axis=0,
            concat_axis=0,
            tiled=True,
        ),
    )
    routed = routed.reshape(experts * capacity, model_width)
    routed_cot = routed_cot.reshape(experts * capacity, model_width)
    gate_proj = jnp.dot(routed, gate_matrix, preferred_element_type=jnp.float32)
    up_proj = jnp.dot(routed, up_matrix, preferred_element_type=jnp.float32)
    hidden_state = (jax.nn.silu(gate_proj) * up_proj).astype(jnp.bfloat16)
    down_part = jnp.dot(hidden_state, down_weight, preferred_element_type=jnp.float32)
    expert_sum = lax.psum_scatter(
        down_part.astype(jnp.bfloat16), "tensor", scatter_dimension=1, tiled=True
    )
    expert_output = expert_sum.reshape(experts, capacity, slice_width)
    returned = lax.all_to_all(
        expert_output, "expert", split_axis=0, concat_axis=0, tiled=True
    ).reshape(experts * capacity, slice_width)
    chosen = returned[target].astype(jnp.float32).reshape(tok_rows, TOPK, slice_width)
    mixed = jnp.sum(route_weights[:, :, None] * chosen, axis=1).astype(jnp.bfloat16)
    route_part = jnp.sum(cotangent.astype(jnp.float32)[:, None, :] * chosen, axis=2)
    grad_route = lax.psum(route_part, "tensor")
    d_hidden = lax.dot_general(
        routed_cot, down_weight, ROW_PAIRS, preferred_element_type=jnp.float32
    )
    grad_down = lax.dot_general(
        hidden_state, routed_cot, COLUMN_PAIRS, preferred_element_type=jnp.float32
    ).astype(jnp.bfloat16)
    sigmoid_gate = jax.nn.sigmoid(gate_proj)
    gate_gradient = (
        d_hidden * up_proj * sigmoid_gate * (1.0 + gate_proj * (1.0 - sigmoid_gate))
    ).astype(jnp.bfloat16)
    up_gradient = (d_hidden * jax.nn.silu(gate_proj)).astype(jnp.bfloat16)
    grad_gate = lax.dot_general(
        routed, gate_gradient, COLUMN_PAIRS, preferred_element_type=jnp.float32
    ).astype(jnp.bfloat16)
    grad_up = lax.dot_general(
        routed, up_gradient, COLUMN_PAIRS, preferred_element_type=jnp.float32
    ).astype(jnp.bfloat16)
    back_part = lax.dot_general(
        gate_gradient, gate_matrix, ROW_PAIRS, preferred_element_type=jnp.float32
    )
    back_part = back_part + lax.dot_general(
        up_gradient, up_matrix, ROW_PAIRS, preferred_element_type=jnp.float32
    )
    input_sum = lax.psum_scatter(
        back_part.astype(jnp.bfloat16), "tensor", scatter_dimension=1, tiled=True
    )
    input_rows = input_sum.reshape(experts, capacity, slice_width)
    returned_grads = lax.all_to_all(
        input_rows, "expert", split_axis=0, concat_axis=0, tiled=True
    ).reshape(experts * capacity, slice_width)
    chosen_grads = returned_grads[target].astype(jnp.float32).reshape(tok_rows, TOPK, slice_width)
    grad_tokens = jnp.sum(route_weights[:, :, None] * chosen_grads, axis=1).astype(jnp.bfloat16)
    return (mixed, grad_tokens, grad_route, grad_gate[None], grad_up[None], grad_down[None])


def over(bits):
    even, odd = bits

    def work(value):
        pairs = [(i, i ^ (odd if i % 2 else even)) for i in range(lax.axis_size("expert"))]
        return lax.ppermute(value, "expert", pairs)

    return work


over_core, over_x, over_y, over_xy = over((1, 1)), over((2, 4)), over((4, 2)), over((6, 6))


def along_z(hops):
    def work(value):
        count = lax.axis_size("tensor")
        return lax.ppermute(value, "tensor", [(i, (i + hops) % count) for i in range(count)])

    return work


over_z = along_z(1)


def dot(a, b, dims=(((1,), (0,)), ((), ()))):
    return lax.dot_general(a, b, dims, preferred_element_type=jnp.float32)


def as_bf16(value):
    return value.astype(jnp.bfloat16)


def as_f32(value):
    return value.astype(jnp.float32)


def beside(*values):
    return jnp.concatenate(values, axis=1)


def below(*values):
    return jnp.concatenate(values, axis=0)


START = {
    "t": (0, 4, 8),
    "tx": (0, 8, 9, 12),
    "ty": (1, 3, 7, 11),
    "td": (4, 13, 10, 14),
    "c": (2, 6, 12),
    "cx": (2, 19, 17, 16),
    "cy": (18, 5, 14, 15),
    "cd": (6, 10, 16, 19),
    "mx": (21, 25, 35, 36),
    "my": (22, 27, 23, 39),
    "mf": (21, 24, 23, 26),
    "mz": (25, 31, 38),
    "gx": (29, 31, 34, 38),
    "gy": (28, 33, 32, 40),
    "gf": (27, 30, 29, 37),
    "gz": (33, 36, 40),
}
ROUTE = {"t": "xyxz", "c": "yzzz", "m": "zxzy", "g": "zxzx"}
HOLD, PAIRED, INNER = 2, 16, (37, 40)


class Rounds:
    def __init__(self, given):
        self.steps, self.values, self.made, self.free = [], dict(given), dict(given), []

    def add(self, start, name, work, *reads, due=None):
        self.steps.append((start, start if due is None else due, name, work, reads))

    def add_free(self, name, work, *reads):
        self.free.append((name, work, reads))

    def run(self, results):
        values, waiting = self.values, {}
        last = max(step[1] for step in self.steps)
        for now in range(last + 1):
            for start, due, name, work, reads in self.steps:
                if start == now:
                    made = self.made[name] = work(*[values[r] for r in reads])
                    if due > now:
                        waiting[name] = (due, made)
                    else:
                        values[name] = made
            for name in [n for n, (due, _) in waiting.items() if due == now]:
                values[name] = waiting.pop(name)[1]
            if now == last:
                break
            needed = {r for start, _, _, _, reads in self.steps if start > now for r in reads} | set(results)
            needed -= {name for name, _, _ in self.free}
            live = [n for n in values if n in needed]
            held = lax.optimization_barrier([values[n] for n in live])
            values.update(zip(live, held, strict=True))
        for name, work, reads in self.free:
            values[name] = work(*[self.made[r] for r in reads])
        return [values[name] for name in results]


def kernel_params():
    return dict(
        compiler_params=pltpu.CompilerParams(vmem_limit_bytes=60 * 2**20),
        cost_estimate=pl.CostEstimate(flops=1, bytes_accessed=1, transcendentals=0),
    )


ANY = pl.BlockSpec(memory_space=pl.ANY)
VMEM = pl.BlockSpec(memory_space=pltpu.VMEM)
SMEM = pl.BlockSpec(memory_space=pltpu.SMEM)


def part_at(place_ref, step, count):
    return lax.rem(place_ref[0] + 2 * count - step, count)


def span(part, width):
    return pl.ds(pl.multiple_of(part * width, 128), width)


def read_parts(pieces, weights, axis, place_ref, first, buffers, sems):
    rows_buffer, weight_buffer = buffers
    copies, count = [], weight_buffer.shape[0] if weights else rows_buffer.shape[0]
    for k in range(count):
        mine = []
        if pieces:
            rows, width = pieces[k][0].shape
            for b, piece in enumerate(pieces[k]):
                mine.append((piece, rows_buffer.at[k, b * rows : (b + 1) * rows, :]))
        start = 0
        for weight in weights:
            if len(weight.shape) == 3:
                weight = weight.at[1 - place_ref[1]]
            side = weight.shape[1 - axis]
            width = weight.shape[axis] // count
            at = span(part_at(place_ref, k + first, count), width)
            if axis == 0:
                mine.append((weight.at[at, :], weight_buffer.at[k, :, start : start + side]))
            else:
                mine.append((weight.at[:, at], weight_buffer.at[k, start : start + side, :]))
            start += side
        mine = [pltpu.make_async_copy(*pair, sems.at[k, i]) for i, pair in enumerate(mine)]
        for copy in mine:
            copy.start()
        copies.append(mine)
    return copies


def summed_product(pieces, weights, axis, place, extras, finish, outs):
    count, blocks, kinds = len(pieces), len(pieces[0]), len(weights)
    rows, width = pieces[0][0].shape
    sides = sum(w.shape[-2:][1 - axis] for w in weights)
    dims = (((1,), (axis,)), ((), ()))

    def body(place_ref, *refs):
        flat, factors = refs[: count * blocks], refs[count * blocks : count * blocks + kinds]
        more = refs[count * blocks + kinds : count * blocks + kinds + len(extras)]
        results = refs[count * blocks + kinds + len(extras) : -4]
        rows_buffer, weight_buffer, total, sems = refs[-4:]
        grid = [flat[k * blocks : (k + 1) * blocks] for k in range(count)]
        steps = read_parts(grid, factors, axis, place_ref, 0, (rows_buffer, weight_buffer), sems)
        for k, copies in enumerate(steps):
            for copy in copies:
                copy.wait()
            value = dot(rows_buffer[k], weight_buffer[k], dims)
            total[...] = value if k == 0 else total[...] + value
        finish(total, more, results)

    return pl.pallas_call(
        body,
        in_specs=[SMEM] + [ANY] * (count * blocks + kinds) + [VMEM] * len(extras),
        out_specs=[VMEM] * len(outs),
        out_shape=outs,
        scratch_shapes=[
            pltpu.VMEM((count, blocks * rows, width), jnp.bfloat16),
            pltpu.VMEM((count, width, sides) if axis == 0 else (count, sides, width), jnp.bfloat16),
            pltpu.VMEM((blocks * rows, sides), jnp.float32),
            pltpu.SemaphoreType.DMA((count, blocks + kinds)),
        ],
        **kernel_params(),
    )(place, *[p for step in pieces for p in step], *weights, *extras)


def block_terms(left, weights, axis, place, count, blocks):
    rows, sides = left.shape[0] // blocks, left.shape[1]
    kinds, width = len(weights), weights[0].shape[axis] // count
    dims = (((1,), (1 - axis,)), ((), ()))

    def body(place_ref, left_ref, *refs):
        factors, outs = refs[:kinds], refs[kinds : kinds + count * blocks]
        weight_buffer, made, sems, out_sems = refs[kinds + count * blocks :]
        steps = read_parts(None, factors, axis, place_ref, 1, (None, weight_buffer), sems)
        sent = []
        for k, copies in enumerate(steps):
            for copy in copies:
                copy.wait()
            made[k] = as_bf16(dot(left_ref[...], weight_buffer[k], dims))
            for b in range(blocks):
                block = made.at[k, b * rows : (b + 1) * rows, :]
                copy = pltpu.make_async_copy(block, outs[k * blocks + b], out_sems.at[k, b])
                copy.start()
                sent.append(copy)
        for copy in sent:
            copy.wait()

    return pl.pallas_call(
        body,
        in_specs=[SMEM, VMEM] + [ANY] * kinds,
        out_specs=[ANY] * (count * blocks),
        out_shape=[jax.ShapeDtypeStruct((rows, width), jnp.bfloat16)] * (count * blocks),
        scratch_shapes=[
            pltpu.VMEM((count, width, sides) if axis == 0 else (count, sides, width), jnp.bfloat16),
            pltpu.VMEM((count, blocks * rows, width), jnp.bfloat16),
            pltpu.SemaphoreType.DMA((count, kinds)),
            pltpu.SemaphoreType.DMA((count, blocks)),
        ],
        **kernel_params(),
    )(place, left, *weights)


def weight_grads(pieces, left, place, kinds, tall):
    count, blocks = len(pieces), len(pieces[0])
    rows, width = pieces[0][0].shape
    side = left.shape[1]
    units = side // (2 * kinds)
    out = (2, units, count * width) if tall else (2, count * width, units)

    def body(place_ref, left_ref, *refs):
        flat, results = refs[: count * blocks], refs[count * blocks : -4]
        rows_buffer, made, sems, out_sems = refs[-4:]
        grid = [flat[k * blocks : (k + 1) * blocks] for k in range(count)]
        steps = read_parts(grid, [], 0, place_ref, 0, (rows_buffer, None), sems)
        sent = []
        for k in range(count):
            for copy in steps[k]:
                copy.wait()
            pair = (left_ref[...], rows_buffer[k]) if tall else (rows_buffer[k], left_ref[...])
            made[k] = as_bf16(dot(*pair, COLUMN_PAIRS))
            at = span(part_at(place_ref, k, count), width)
            for i in range(2 * kinds):
                cut = pl.ds(i * units, units)
                core = place_ref[1] if i < kinds else 1 - place_ref[1]
                result = results[i % kinds].at[core]
                if tall:
                    pair = made.at[k, cut, :], result.at[:, at]
                else:
                    pair = made.at[k, :, cut], result.at[at, :]
                copy = pltpu.make_async_copy(*pair, out_sems.at[k, i])
                copy.start()
                sent.append(copy)
        for copy in sent:
            copy.wait()

    return pl.pallas_call(
        body,
        in_specs=[SMEM, VMEM] + [ANY] * (count * blocks),
        out_specs=[ANY] * kinds,
        out_shape=[jax.ShapeDtypeStruct(out, jnp.bfloat16)] * kinds,
        scratch_shapes=[
            pltpu.VMEM((count, blocks * rows, width), jnp.bfloat16),
            pltpu.VMEM((count, side, width) if tall else (count, width, side), jnp.bfloat16),
            pltpu.SemaphoreType.DMA((count, blocks)),
            pltpu.SemaphoreType.DMA((count, 2 * kinds)),
        ],
        **kernel_params(),
    )(place, left, *[p for step in pieces for p in step])


def chip_plan(tokens, route_ids, route_weights, cotangent, w_gate, w_up, w_down):
    count = lax.axis_size("tensor")
    experts = lax.axis_size("expert")
    place, me = lax.axis_index("tensor"), lax.axis_index("expert")
    place_at = jnp.stack([place, me % 2])
    rows, width = tokens.shape
    units = w_gate.shape[2]

    labels = jnp.arange(experts, dtype=jnp.int32)
    named = route_ids[:, :, None] == labels[None, None, :]
    shares = jnp.sum(jnp.where(named, route_weights[:, :, None], 0.0), axis=1)

    def part_of(step):
        return lax.rem(place + 2 * count - step, count)

    r = Rounds(
        {
            ("t", 0): tokens,
            ("c", 0): cotangent,
            "w": shares,
            "G": w_gate[0],
            "U": w_up[0],
            "D": w_down[0],
        }
    )

    def transfer(at, name, work, read):
        r.add(at, name, work, read, due=at + HOLD)
        return at + HOLD + 1

    ready, pieces = {}, {}
    for a in "tc":
        ready[a] = 0
        for k in range(count):
            if k < count - 1:
                transfer(START[a][k], (a, k + 1), over_z, (a, k))
            work, read = {
                "x": (over_x, (a + "y", k)),
                "y": (over_y, (a + "x", k)),
                "z": (over_z, (a + "d", k - 1)),
            }[ROUTE[a][k]]
            ready[a] = max(
                ready[a],
                transfer(START[a + "x"][k], (a + "x", k), over_x, (a, k)),
                transfer(START[a + "y"][k], (a + "y", k), over_y, (a, k)),
                transfer(START[a + "d"][k], (a + "d", k), work, read),
            )
        pieces[a] = [(a + which, k) if which else (a, k) for k in range(count) for which in ("", "x", "y", "d")]
    m_at, g_at = ready["t"], max(ready["c"], ready["t"] + 2)

    cores = [[i, i + 1] for i in range(0, experts, 2)]
    for name in "GUD":
        r.add(0, name + "s", lambda w: lax.all_gather(w, "expert", axis_index_groups=cores), name, due=PAIRED)
    wides, talls = ("G", "U", "Gs", "Us"), ("D", "Ds")
    for name, work in zip(("wx", "wy", "wd"), (over_x, over_y, over_xy), strict=True):
        r.add(0, name, work, "w")

    def share_pair(*blocks):
        share = below(*blocks)
        return beside(*[lax.dynamic_slice_in_dim(share, me ^ i, 1, 1) for i in range(2)])

    r.add(6, "s", share_pair, "w", "wx", "wy", "wd")

    def sizes(dtype, *columns):
        return [jax.ShapeDtypeStruct((4 * rows, n), dtype) for n in columns]

    def activations(total, extras, outs):
        share, both, weighted = extras[0][...], *outs
        both[...] = total[...]
        for i in range(2):
            gate = total[:, 2 * i * units : (2 * i + 1) * units]
            up = total[:, (2 * i + 1) * units : (2 * i + 2) * units]
            value = share[:, i : i + 1] * (gate * jax.nn.sigmoid(gate) * up)
            weighted[:, i * units : (i + 1) * units] = as_bf16(value)

    def gradients(total, extras, outs):
        share, both = extras[0][...], extras[1]
        to_tokens, to_weights, inner = outs
        for i in range(2):
            gate = both[:, 2 * i * units : (2 * i + 1) * units]
            up = both[:, (2 * i + 1) * units : (2 * i + 2) * units]
            d_plain = total[:, i * units : (i + 1) * units]
            weight = share[:, i : i + 1]
            sigmoid_gate = jax.nn.sigmoid(gate)
            silu_gate = gate * sigmoid_gate
            inner[:, i : i + 1] = jnp.sum(silu_gate * up * d_plain, axis=1, keepdims=True)
            d_hidden = weight * d_plain
            d_gate = d_hidden * up * sigmoid_gate * (1.0 + gate * (1.0 - sigmoid_gate))
            d_up = d_hidden * silu_gate
            to_weights[:, 2 * i * units : (2 * i + 1) * units] = as_bf16(d_gate)
            to_weights[:, (2 * i + 1) * units : (2 * i + 2) * units] = as_bf16(d_up)
            to_tokens[:, 2 * i * units : (2 * i + 1) * units] = as_bf16(weight * d_gate)
            to_tokens[:, (2 * i + 1) * units : (2 * i + 2) * units] = as_bf16(weight * d_up)

    def steps_of(values):
        return [values[4 * k : 4 * k + 4] for k in range(count)]

    def forward(share, *values):
        outs = sizes(jnp.float32, 4 * units) + sizes(jnp.bfloat16, 2 * units)
        parts, weights = steps_of(values), values[4 * count :]
        return summed_product(parts, weights, 0, place_at, [share], activations, outs)

    def backward(share, both, *values):
        outs = sizes(jnp.bfloat16, 4 * units, 4 * units) + sizes(jnp.float32, 2)
        parts, weights = steps_of(values), values[4 * count :]
        return summed_product(parts, weights, 1, place_at, [share, both], gradients, outs)

    def unpacked(at, name, work, names, *reads):
        r.add(at, name, work, *reads)
        for i, part in enumerate(names):
            r.add(at, part, lambda v, i=i: v[i], name)

    unpacked(m_at, "H", forward, ("h", "v"), "s", *pieces["t"], *wides)
    unpacked(g_at, "E", backward, ("g", "b", "i"), "s", "h", *pieces["c"], *talls)

    for at, o, left, weights, axis in (
        (m_at + 1, "m", "v", talls, 1),
        (g_at + 1, "g", "g", wides, 0),
    ):

        def work(left, *weights, axis=axis):
            return block_terms(left, weights, axis, place_at, count, 4)

        names = [(o + "p", k, b) for k in range(count) for b in range(4)]
        unpacked(at, o + "P", work, names, left, *weights)

    def term(at, name, o, k, block, *more):
        def work(mine, *more):
            return as_bf16(sum([as_f32(v) for v in more], as_f32(mine))) if more else mine

        r.add(at, name, work, (o + "p", k, block), *more)

    own, side, front, far = range(4)
    for o in "mg":
        for k in range(count):
            came = [(o + "f", k - 1)] if k and ROUTE[o][k - 1] == "z" else []
            for which, work, block in (("f", None, far), ("x", over_x, side), ("y", over_y, front)):
                if which == "f":
                    work, more = {"x": over_x, "y": over_y, "z": over_z}[ROUTE[o][k]], came
                else:
                    more = [(o + "f", k)] if ROUTE[o][k] == ("y" if which == "x" else "x") else []
                at = START[o + which][k]
                term(at, (o + which + "s", k), o, k, block, *more)
                ready[o + which] = transfer(at, (o + which, k), work, (o + which + "s", k))
            at = START[o + "z"][k] if k < count - 1 else 0
            more = [(o + "x", k), (o + "y", k)] + ([(o + "z", k - 1)] if k else [])
            at = at or max(ready[o + "x"], ready[o + "y"], ready[o + "z"])
            term(at, (o + "s", k), o, k, own, *more)
            if k < count - 1:
                ready[o + "z"] = transfer(at, (o + "z", k), over_z, (o + "s", k))

    for q, work in enumerate((over_x, over_y, over_xy), 1):
        r.add(INNER[0], ("n", q), lambda v, work=work, q=q: work(v[q * rows : (q + 1) * rows]), "i")

    def route_sums(inner, *others):
        total = 0.0
        first = jnp.where(me % 2 == 1, 4, 2)
        for bits, found in zip((0, first, 6 - first, 6), (inner[:rows], *others), strict=True):
            for i in range(2):
                total += jnp.where(route_ids == me ^ bits ^ i, found[:, i : i + 1], 0.0)
        return total

    r.add(INNER[0] + 1, ("o", 0), route_sums, "i", *[("n", q) for q in (1, 2, 3)])
    for k in range(1, count):
        r.add(INNER[1], ("o", k), along_z(k), ("o", 0))

    def in_order(*turns):
        turns = jnp.stack(turns)
        return sum(lax.dynamic_index_in_dim(turns, part_of(k), 0, False) for k in range(count))

    r.add(INNER[1] + 1, "o", in_order, *[("o", k) for k in range(count)])

    def summed(*terms):
        return [
            lax.psum_scatter(v, "expert", scatter_dimension=0, axis_index_groups=cores) for v in terms
        ]

    def tall_grads(left, *parts):
        return summed(*weight_grads(steps_of(parts), left, place_at, 1, True))

    def wide_grads(left, *parts):
        return summed(*weight_grads(steps_of(parts), left, place_at, 2, False))

    r.add_free("A", tall_grads, "v", *pieces["c"])
    r.add_free("B", wide_grads, "b", *pieces["t"])
    last = count - 1
    mixed, grad_tokens, grad_route, wide, tall = r.run([("ms", last), ("gs", last), "o", "B", "A"])
    return mixed, grad_tokens, grad_route, wide[0][None], wide[1][None], tall[0][None]


def local(tokens, route_ids, route_weights, cotangent, w_gate, w_up, w_down):
    experts = lax.axis_size("expert")
    capacity = 4 * tokens.shape[0] // experts
    whole = 2 * capacity >= tokens.shape[0] and (experts, lax.axis_size("tensor")) == (8, 4)
    plan = chip_plan if whole else slot_plan
    return plan(tokens, route_ids, route_weights, cotangent, w_gate, w_up, w_down)


def solution(mesh):
    placed = (
        P("expert", "tensor"),
        P("expert", None),
        P("expert", None),
        P("expert", "tensor"),
        P("expert", None, "tensor"),
        P("expert", None, "tensor"),
        P("expert", "tensor", None),
    )
    return jax.shard_map(
        local,
        mesh=mesh,
        in_specs=placed,
        out_specs=(
            P("expert", "tensor"),
            P("expert", "tensor"),
            P("expert", None),
            P("expert", None, "tensor"),
            P("expert", None, "tensor"),
            P("expert", "tensor", None),
        ),
        check_vma=False,
    )
```

```python
import jax
import jax.numpy as jnp
from jax import lax
from jax.experimental import pallas as pl
from jax.experimental.pallas import tpu as pltpu
from jax.sharding import PartitionSpec as P

TOPK = 2


ROW_PAIRS = (((1,), (1,)), ((), ()))
COLUMN_PAIRS = (((0,), (0,)), ((), ()))


def slot_tables(route_ids, experts, capacity):
    pair_count = route_ids.shape[0] * route_ids.shape[1]
    flat_ids = route_ids.reshape(pair_count)
    labels = jnp.arange(experts, dtype=jnp.int32)
    onehot = (flat_ids[:, None] == labels[None, :]).astype(jnp.int32)
    before = jnp.cumsum(onehot, axis=0) - onehot
    slot_index = jnp.sum(before * onehot, axis=1)
    target = flat_ids * capacity + slot_index
    source = (
        jnp.full((experts * capacity,), pair_count, jnp.int32)
        .at[target]
        .set(jnp.arange(pair_count, dtype=jnp.int32))
    )
    return (target, source)


def fill_slots(token_part, cot_part, weight_flat, source):
    row_of = source // TOPK
    zero_row = jnp.zeros((1, token_part.shape[1]), jnp.bfloat16)
    padded_tokens = jnp.concatenate([token_part, zero_row], axis=0)
    padded_cot = jnp.concatenate([cot_part, zero_row], axis=0)
    padded_weight = jnp.concatenate([weight_flat, jnp.zeros((1,), jnp.float32)], axis=0)
    token_slots = padded_tokens[row_of]
    cot_slots = (padded_weight[source][:, None] * padded_cot[row_of].astype(jnp.float32)).astype(
        jnp.bfloat16
    )
    return (token_slots, cot_slots)


def slot_plan(tokens, route_ids, route_weights, cotangent, w_gate, w_up, w_down):
    experts = lax.axis_size("expert")
    tok_rows, slice_width = tokens.shape
    capacity = 4 * tok_rows // experts
    gate_matrix = w_gate[0]
    up_matrix = w_up[0]
    down_weight = w_down[0]
    target, source = slot_tables(route_ids, experts, capacity)
    weight_flat = route_weights.reshape(tok_rows * TOPK)
    full_tokens, full_cot = (
        lax.all_gather(tokens, "tensor", axis=1, tiled=True),
        lax.all_gather(cotangent, "tensor", axis=1, tiled=True),
    )
    model_width = full_tokens.shape[1]
    token_slots, cot_slots = fill_slots(full_tokens, full_cot, weight_flat, source)
    routed, routed_cot = (
        lax.all_to_all(
            token_slots.reshape(experts, capacity, model_width),
            "expert",
            split_axis=0,
            concat_axis=0,
            tiled=True,
        ),
        lax.all_to_all(
            cot_slots.reshape(experts, capacity, model_width),
            "expert",
            split_axis=0,
            concat_axis=0,
            tiled=True,
        ),
    )
    routed = routed.reshape(experts * capacity, model_width)
    routed_cot = routed_cot.reshape(experts * capacity, model_width)
    gate_proj = jnp.dot(routed, gate_matrix, preferred_element_type=jnp.float32)
    up_proj = jnp.dot(routed, up_matrix, preferred_element_type=jnp.float32)
    hidden_state = (jax.nn.silu(gate_proj) * up_proj).astype(jnp.bfloat16)
    down_part = jnp.dot(hidden_state, down_weight, preferred_element_type=jnp.float32)
    expert_sum = lax.psum_scatter(
        down_part.astype(jnp.bfloat16), "tensor", scatter_dimension=1, tiled=True
    )
    expert_output = expert_sum.reshape(experts, capacity, slice_width)
    returned = lax.all_to_all(
        expert_output, "expert", split_axis=0, concat_axis=0, tiled=True
    ).reshape(experts * capacity, slice_width)
    chosen = returned[target].astype(jnp.float32).reshape(tok_rows, TOPK, slice_width)
    mixed = jnp.sum(route_weights[:, :, None] * chosen, axis=1).astype(jnp.bfloat16)
    route_part = jnp.sum(cotangent.astype(jnp.float32)[:, None, :] * chosen, axis=2)
    grad_route = lax.psum(route_part, "tensor")
    d_hidden = lax.dot_general(
        routed_cot, down_weight, ROW_PAIRS, preferred_element_type=jnp.float32
    )
    grad_down = lax.dot_general(
        hidden_state, routed_cot, COLUMN_PAIRS, preferred_element_type=jnp.float32
    ).astype(jnp.bfloat16)
    sigmoid_gate = jax.nn.sigmoid(gate_proj)
    gate_gradient = (
        d_hidden * up_proj * sigmoid_gate * (1.0 + gate_proj * (1.0 - sigmoid_gate))
    ).astype(jnp.bfloat16)
    up_gradient = (d_hidden * jax.nn.silu(gate_proj)).astype(jnp.bfloat16)
    grad_gate = lax.dot_general(
        routed, gate_gradient, COLUMN_PAIRS, preferred_element_type=jnp.float32
    ).astype(jnp.bfloat16)
    grad_up = lax.dot_general(
        routed, up_gradient, COLUMN_PAIRS, preferred_element_type=jnp.float32
    ).astype(jnp.bfloat16)
    back_part = lax.dot_general(
        gate_gradient, gate_matrix, ROW_PAIRS, preferred_element_type=jnp.float32
    )
    back_part = back_part + lax.dot_general(
        up_gradient, up_matrix, ROW_PAIRS, preferred_element_type=jnp.float32
    )
    input_sum = lax.psum_scatter(
        back_part.astype(jnp.bfloat16), "tensor", scatter_dimension=1, tiled=True
    )
    input_rows = input_sum.reshape(experts, capacity, slice_width)
    returned_grads = lax.all_to_all(
        input_rows, "expert", split_axis=0, concat_axis=0, tiled=True
    ).reshape(experts * capacity, slice_width)
    chosen_grads = returned_grads[target].astype(jnp.float32).reshape(tok_rows, TOPK, slice_width)
    grad_tokens = jnp.sum(route_weights[:, :, None] * chosen_grads, axis=1).astype(jnp.bfloat16)
    return (mixed, grad_tokens, grad_route, grad_gate[None], grad_up[None], grad_down[None])


def over(bits):
    even, odd = bits

    def work(value):
        pairs = [(i, i ^ (odd if i % 2 else even)) for i in range(lax.axis_size("expert"))]
        return lax.ppermute(value, "expert", pairs)

    return work


over_core, over_x, over_y, over_xy = over((1, 1)), over((2, 4)), over((4, 2)), over((6, 6))


def along_z(hops):
    def work(value):
        count = lax.axis_size("tensor")
        return lax.ppermute(value, "tensor", [(i, (i + hops) % count) for i in range(count)])

    return work


over_z = along_z(1)


def dot(a, b, dims=(((1,), (0,)), ((), ()))):
    return lax.dot_general(a, b, dims, preferred_element_type=jnp.float32)


def as_bf16(value):
    return value.astype(jnp.bfloat16)


def as_f32(value):
    return value.astype(jnp.float32)


def beside(*values):
    return jnp.concatenate(values, axis=1)


def below(*values):
    return jnp.concatenate(values, axis=0)


START = {
    "t": (0, 4, 8),
    "tx": (0, 8, 9, 12),
    "ty": (1, 3, 7, 11),
    "td": (4, 13, 10, 14),
    "c": (2, 6, 12),
    "cx": (2, 19, 17, 16),
    "cy": (18, 5, 14, 15),
    "cd": (6, 10, 16, 19),
}
ROUTE = {"t": "xyxz", "c": "yzzz"}
SUMS = {
    "mx0": (21, 22), "my0": (21, 22), "mf0": (21, 22), "mx1": (21, 23), "my1": (21, 23),
    "mf1": (23, 23), "mf2": (24, 25), "my2": (26, 26), "mx3": (27, 28),
    "mz": ((23, 23), (24, 25), (27, 28), (30, 30)),
    "gx0": (24, 25), "gy0": (24, 25), "gf0": (24, 25), "gx1": (25, 27), "gy1": (25, 27),
    "gf1": (26, 27), "gf2": (28, 28), "gy2": (29, 29), "gx3": (28, 29),
    "gz": ((26, 27), (28, 29), (30, 30), (31, 31)),
}
KERNELS, GRADS, INNER, HOLD, PAIRED = (19, 20, 22, 23), (26, 25), (27, 29), 2, 16


class Rounds:
    def __init__(self, given):
        self.steps, self.values = [], dict(given)

    def add(self, start, name, work, *reads, due=None):
        self.steps.append((start, start if due is None else due, name, work, reads))

    def run(self, results):
        values, waiting = self.values, {}
        last = max(step[1] for step in self.steps)
        for now in range(last + 1):
            for start, due, name, work, reads in self.steps:
                if start == now:
                    made = work(*[values[r] if r in values else waiting[r][1] for r in reads])
                    if due > now:
                        waiting[name] = (due, made)
                    else:
                        values[name] = made
            for name in [n for n, (due, _) in waiting.items() if due == now]:
                values[name] = waiting.pop(name)[1]
            if now == last:
                break
            needed = {r for start, _, _, _, reads in self.steps if start > now for r in reads} | set(results)
            live = [n for n in values if n in needed]
            held = lax.optimization_barrier([values[n] for n in live])
            values.update(zip(live, held, strict=True))
        return [values[name] for name in results]


def kernel_params():
    return dict(
        compiler_params=pltpu.CompilerParams(vmem_limit_bytes=60 * 2**20),
        cost_estimate=pl.CostEstimate(flops=1, bytes_accessed=1, transcendentals=0),
    )


ANY = pl.BlockSpec(memory_space=pl.ANY)
VMEM = pl.BlockSpec(memory_space=pltpu.VMEM)
SMEM = pl.BlockSpec(memory_space=pltpu.SMEM)


def part_at(place_ref, step, count):
    return lax.rem(place_ref[0] + 2 * count - step, count)


def span(part, width):
    return pl.ds(pl.multiple_of(part * width, 128), width)


def read_parts(pieces, weights, axis, place_ref, first, buffers, sems):
    rows_buffer, weight_buffer = buffers
    copies, count = [], weight_buffer.shape[0] if weights else rows_buffer.shape[0]
    for k in range(count):
        mine = []
        if pieces:
            rows, width = pieces[k][0].shape
            for b, piece in enumerate(pieces[k]):
                mine.append((piece, rows_buffer.at[k, b * rows : (b + 1) * rows, :]))
        start = 0
        for weight in weights:
            if len(weight.shape) == 3:
                weight = weight.at[1 - place_ref[1]]
            side = weight.shape[1 - axis]
            width = weight.shape[axis] // count
            at = span(part_at(place_ref, k + first, count), width)
            if axis == 0:
                mine.append((weight.at[at, :], weight_buffer.at[k, :, start : start + side]))
            else:
                mine.append((weight.at[:, at], weight_buffer.at[k, start : start + side, :]))
            start += side
        mine = [pltpu.make_async_copy(*pair, sems.at[k, i]) for i, pair in enumerate(mine)]
        for copy in mine:
            copy.start()
        copies.append(mine)
    return copies


def summed_product(pieces, weights, axis, place, extras, finish, outs):
    count, blocks, kinds = len(pieces), len(pieces[0]), len(weights)
    rows, width = pieces[0][0].shape
    sides = sum(w.shape[-2:][1 - axis] for w in weights)
    dims = (((1,), (axis,)), ((), ()))

    def body(place_ref, *refs):
        flat, factors = refs[: count * blocks], refs[count * blocks : count * blocks + kinds]
        more = refs[count * blocks + kinds : count * blocks + kinds + len(extras)]
        results = refs[count * blocks + kinds + len(extras) : -4]
        rows_buffer, weight_buffer, total, sems = refs[-4:]
        grid = [flat[k * blocks : (k + 1) * blocks] for k in range(count)]
        steps = read_parts(grid, factors, axis, place_ref, 0, (rows_buffer, weight_buffer), sems)
        for k, copies in enumerate(steps):
            for copy in copies:
                copy.wait()
            value = dot(rows_buffer[k], weight_buffer[k], dims)
            total[...] = value if k == 0 else total[...] + value
        finish(total, more, results)

    return pl.pallas_call(
        body,
        in_specs=[SMEM] + [ANY] * (count * blocks + kinds) + [VMEM] * len(extras),
        out_specs=[VMEM] * len(outs),
        out_shape=outs,
        scratch_shapes=[
            pltpu.VMEM((count, blocks * rows, width), jnp.bfloat16),
            pltpu.VMEM((count, width, sides) if axis == 0 else (count, sides, width), jnp.bfloat16),
            pltpu.VMEM((blocks * rows, sides), jnp.float32),
            pltpu.SemaphoreType.DMA((count, blocks + kinds)),
        ],
        **kernel_params(),
    )(place, *[p for step in pieces for p in step], *weights, *extras)


def block_terms(left, weights, axis, place, count, layout, blocks):
    rows, sides = left.shape[0] // blocks, left.shape[1]
    kinds, width = len(weights), weights[0].shape[axis] // count
    dims = (((1,), (1 - axis,)), ((), ()))

    def body(place_ref, left_ref, *refs):
        factors, outs = refs[:kinds], refs[kinds : kinds + len(layout)]
        weight_buffer, made, sems, out_sems = refs[kinds + len(layout) :]
        steps = read_parts(None, factors, axis, place_ref, 1, (None, weight_buffer), sems)
        sent = []
        for k, copies in enumerate(steps):
            for copy in copies:
                copy.wait()
            made[k] = as_bf16(dot(left_ref[...], weight_buffer[k], dims))
            for out, listed in zip(outs, layout, strict=True):
                for i, (step, block) in enumerate(listed):
                    if step == k:
                        term = made.at[k, block * rows : (block + 1) * rows, :]
                        copy = pltpu.make_async_copy(
                            term, out.at[i * rows : (i + 1) * rows, :], out_sems.at[k, block]
                        )
                        copy.start()
                        sent.append(copy)
        for copy in sent:
            copy.wait()

    return pl.pallas_call(
        body,
        in_specs=[SMEM, VMEM] + [ANY] * kinds,
        out_specs=[ANY] * len(layout),
        out_shape=[jax.ShapeDtypeStruct((len(out) * rows, width), jnp.bfloat16) for out in layout],
        scratch_shapes=[
            pltpu.VMEM((count, width, sides) if axis == 0 else (count, sides, width), jnp.bfloat16),
            pltpu.VMEM((count, blocks * rows, width), jnp.bfloat16),
            pltpu.SemaphoreType.DMA((count, kinds)),
            pltpu.SemaphoreType.DMA((count, blocks)),
        ],
        **kernel_params(),
    )(place, left, *weights)


def weight_grads(pieces, left, place, kinds, tall):
    count, blocks = len(pieces), len(pieces[0])
    rows, width = pieces[0][0].shape
    side = left.shape[1]
    units = side // (2 * kinds)
    out = (units, count * width) if tall else (2, count * width, units)
    made_outs = 2 if tall else kinds

    def body(place_ref, left_ref, *refs):
        flat, results = refs[: count * blocks], refs[count * blocks : -4]
        rows_buffer, made, sems, out_sems = refs[-4:]
        grid = [flat[k * blocks : (k + 1) * blocks] for k in range(count)]
        steps = read_parts(grid, [], 0, place_ref, 0, (rows_buffer, None), sems)
        sent = []
        for k in range(count):
            for copy in steps[k]:
                copy.wait()
            pair = (left_ref[...], rows_buffer[k]) if tall else (rows_buffer[k], left_ref[...])
            made[k] = as_bf16(dot(*pair, COLUMN_PAIRS))
            at = span(part_at(place_ref, k, count), width)
            for i in range(2 * kinds):
                cut = pl.ds(i * units, units)
                core = place_ref[1] if i < kinds else 1 - place_ref[1]
                if tall:
                    pair = made.at[k, cut, :], results[i].at[:, at]
                else:
                    pair = made.at[k, :, cut], results[i % kinds].at[core, at, :]
                copy = pltpu.make_async_copy(*pair, out_sems.at[k, i])
                copy.start()
                sent.append(copy)
        for copy in sent:
            copy.wait()

    return pl.pallas_call(
        body,
        in_specs=[SMEM, VMEM] + [ANY] * (count * blocks),
        out_specs=[ANY] * made_outs,
        out_shape=[jax.ShapeDtypeStruct(out, jnp.bfloat16)] * made_outs,
        scratch_shapes=[
            pltpu.VMEM((count, blocks * rows, width), jnp.bfloat16),
            pltpu.VMEM((count, side, width) if tall else (count, width, side), jnp.bfloat16),
            pltpu.SemaphoreType.DMA((count, blocks)),
            pltpu.SemaphoreType.DMA((count, 2 * kinds)),
        ],
        **kernel_params(),
    )(place, left, *[p for step in pieces for p in step])


def closing_sum(*terms):
    def body(*refs):
        refs[-1][...] = as_bf16(sum([as_f32(ref[...]) for ref in refs[1:-1]], as_f32(refs[0][...])))

    return pl.pallas_call(
        body,
        in_specs=[VMEM] * len(terms),
        out_specs=VMEM,
        out_shape=jax.ShapeDtypeStruct(terms[0].shape, jnp.bfloat16),
        compiler_params=pltpu.CompilerParams(vmem_limit_bytes=60 * 2**20),
        cost_estimate=pl.CostEstimate(flops=10**11, bytes_accessed=3 * 10**8, transcendentals=0),
    )(*terms)


def chip_plan(tokens, route_ids, route_weights, cotangent, w_gate, w_up, w_down):
    count = lax.axis_size("tensor")
    experts = lax.axis_size("expert")
    place, me = lax.axis_index("tensor"), lax.axis_index("expert")
    place_at = jnp.stack([place, me % 2])
    rows, width = tokens.shape
    units = w_gate.shape[2]

    labels = jnp.arange(experts, dtype=jnp.int32)
    named = route_ids[:, :, None] == labels[None, None, :]
    shares = jnp.sum(jnp.where(named, route_weights[:, :, None], 0.0), axis=1)

    def part_of(step):
        return lax.rem(place + 2 * count - step, count)

    r = Rounds(
        {
            ("t", 0): tokens,
            ("c", 0): cotangent,
            "w": shares,
            "G": w_gate[0],
            "U": w_up[0],
            "D": w_down[0],
        }
    )

    def transfer(at, name, work, read):
        r.add(at, name, work, read, due=at + HOLD)
        return at + HOLD + 1

    ready, pieces = {}, {}
    for a in "tc":
        ready[a] = 0
        for k in range(count):
            if k < count - 1:
                transfer(START[a][k], (a, k + 1), over_z, (a, k))
            work, read = {
                "x": (over_x, (a + "y", k)),
                "y": (over_y, (a + "x", k)),
                "z": (over_z, (a + "d", k - 1)),
            }[ROUTE[a][k]]
            ready[a] = max(
                ready[a],
                transfer(START[a + "x"][k], (a + "x", k), over_x, (a, k)),
                transfer(START[a + "y"][k], (a + "y", k), over_y, (a, k)),
                transfer(START[a + "d"][k], (a + "d", k), work, read),
            )
        pieces[a] = [(a + which, k) if which else (a, k) for k in range(count) for which in ("", "x", "y", "d")]
    m_at, m_terms, g_at, g_terms = KERNELS

    cores = [[i, i + 1] for i in range(0, experts, 2)]
    for name in "GUD":
        r.add(0, name + "s", lambda w: lax.all_gather(w, "expert", axis_index_groups=cores), name, due=PAIRED)
    wides, talls = ("G", "U", "Gs", "Us"), ("D", "Ds")
    for name, work in zip(("wx", "wy", "wd"), (over_x, over_y, over_xy), strict=True):
        r.add(0, name, work, "w")

    def share_pair(*blocks):
        share = below(*blocks)
        return beside(*[lax.dynamic_slice_in_dim(share, me ^ i, 1, 1) for i in range(2)])

    r.add(6, "s", share_pair, "w", "wx", "wy", "wd")

    def sizes(dtype, *columns):
        return [jax.ShapeDtypeStruct((4 * rows, n), dtype) for n in columns]

    def activations(total, extras, outs):
        share, both, weighted = extras[0][...], *outs
        both[...] = total[...]
        for i in range(2):
            gate = total[:, 2 * i * units : (2 * i + 1) * units]
            up = total[:, (2 * i + 1) * units : (2 * i + 2) * units]
            value = share[:, i : i + 1] * (gate * jax.nn.sigmoid(gate) * up)
            weighted[:, i * units : (i + 1) * units] = as_bf16(value)

    def gradients(total, extras, outs):
        share, both = extras[0][...], extras[1]
        to_tokens, to_weights, inner = outs
        for i in range(2):
            gate = both[:, 2 * i * units : (2 * i + 1) * units]
            up = both[:, (2 * i + 1) * units : (2 * i + 2) * units]
            d_plain = total[:, i * units : (i + 1) * units]
            weight = share[:, i : i + 1]
            sigmoid_gate = jax.nn.sigmoid(gate)
            silu_gate = gate * sigmoid_gate
            inner[:, i : i + 1] = jnp.sum(silu_gate * up * d_plain, axis=1, keepdims=True)
            d_hidden = weight * d_plain
            d_gate = d_hidden * up * sigmoid_gate * (1.0 + gate * (1.0 - sigmoid_gate))
            d_up = d_hidden * silu_gate
            to_weights[:, 2 * i * units : (2 * i + 1) * units] = as_bf16(d_gate)
            to_weights[:, (2 * i + 1) * units : (2 * i + 2) * units] = as_bf16(d_up)
            to_tokens[:, 2 * i * units : (2 * i + 1) * units] = as_bf16(weight * d_gate)
            to_tokens[:, (2 * i + 1) * units : (2 * i + 2) * units] = as_bf16(weight * d_up)

    def steps_of(values):
        return [values[4 * k : 4 * k + 4] for k in range(count)]

    def forward(share, *values):
        outs = sizes(jnp.float32, 4 * units) + sizes(jnp.bfloat16, 2 * units)
        parts, weights = steps_of(values), values[4 * count :]
        return summed_product(parts, weights, 0, place_at, [share], activations, outs)

    def backward(share, both, *values):
        outs = sizes(jnp.bfloat16, 4 * units, 4 * units) + sizes(jnp.float32, 2)
        parts, weights = steps_of(values), values[4 * count :]
        return summed_product(parts, weights, 1, place_at, [share, both], gradients, outs)

    def unpacked(at, name, work, names, *reads):
        r.add(at, name, work, *reads)
        for i, part in enumerate(names):
            r.add(at, part, lambda v, i=i: v[i], name)

    unpacked(m_at, "H", forward, ("h", "v"), "s", *pieces["t"], *wides)
    unpacked(g_at, "E", backward, ("g", "b", "i"), "s", "h", *pieces["c"], *talls)

    own, side, front, far = range(4)
    layout = {
        "x0": [(0, side)],
        "y0": [(0, front)],
        "x1": [(1, side), (2, side)],
        "y1": [(1, front), (3, front), (3, far)],
        "f0": [(0, far)],
        "f1": [(1, far)],
        "f2": [(2, far)],
        "x3": [(3, side)],
        "y2": [(2, front)],
    }
    layout |= {k: [(k, own)] for k in range(count)}

    def cut(value, n):
        return value[n * rows : (n + 1) * rows]

    def add_up(*terms):
        return as_bf16(sum([as_f32(v) for v in terms[1:]], as_f32(terms[0])))

    for o, at, left, weights, axis in (("m", m_terms, "v", talls, 1), ("g", g_terms, "g", wides, 0)):

        def work(left, *weights, axis=axis):
            return block_terms(left, weights, axis, place_at, count, list(layout.values()), 4)

        unpacked(at, o + "P", work, [(o + "p", name) for name in layout], left, *weights)

        def send(name, work, terms, *reads, o=o):
            start, due = SUMS[o + name]
            r.add(start, (o + "s", name), terms, (o + "p", name), *[(o, n) for n in reads])
            r.add(start, (o, name), work, (o + "s", name), due=due)

        for name, work in (("x0", over_x), ("y0", over_y), ("f0", over_z), ("x1", over_x), ("y1", over_y)):
            send(name, work, lambda v: v)
        send("f1", over_z, add_up, "f0")
        send("f2", over_x, add_up, "f1")
        send("y2", over_y, add_up, "f2")
        send("x3", over_x, lambda v, y: add_up(v, cut(y, 2)), "y1")

        def send_own(k, terms, *reads, o=o):
            start, due = SUMS[o + "z"][k]
            add = closing_sum if (o, k) == ("g", 3) else add_up
            r.add(start, (o + "s", k), lambda *v: add(*terms(*v)), (o + "p", k), *[(o, n) for n in reads])
            if k < count - 1:
                r.add(start, (o, k), over_z, (o + "s", k), due=due)

        send_own(0, lambda v, x, y: (v, x, y), "x0", "y0")
        send_own(1, lambda v, x, y, z: (v, cut(x, 0), cut(y, 0), z), "x1", "y1", 0)
        send_own(2, lambda v, x, y, z: (v, cut(x, 1), y, z), "x1", "y2", 1)
        send_own(3, lambda v, x, y, z: (v, x, cut(y, 1), z), "x3", "y1", 2)

    for q, work in enumerate((over_x, over_y, over_xy), 1):
        r.add(INNER[0], ("n", q), lambda v, work=work, q=q: work(v[q * rows : (q + 1) * rows]), "i")

    def route_sums(inner, *others):
        total = 0.0
        first = jnp.where(me % 2 == 1, 4, 2)
        for bits, found in zip((0, first, 6 - first, 6), (inner[:rows], *others), strict=True):
            for i in range(2):
                total += jnp.where(route_ids == me ^ bits ^ i, found[:, i : i + 1], 0.0)
        return total

    r.add(INNER[0] + 1, ("o", 0), route_sums, "i", *[("n", q) for q in (1, 2, 3)])
    for k in range(1, count):
        r.add(INNER[1], ("o", k), along_z(k), ("o", 0))

    def in_order(*turns):
        turns = jnp.stack(turns)
        return sum(lax.dynamic_index_in_dim(turns, part_of(k), 0, False) for k in range(count))

    r.add(INNER[1] + 1, "o", in_order, *[("o", k) for k in range(count)])

    def tall_terms(left, *parts):
        return weight_grads(steps_of(parts), left, place_at, 1, True)

    def wide_terms(left, *parts):
        return weight_grads(steps_of(parts), left, place_at, 2, False)

    def summed(*terms):
        return [
            lax.psum_scatter(v, "expert", scatter_dimension=0, axis_index_groups=cores) for v in terms
        ]

    end = max(step[1] for step in r.steps)
    unpacked(GRADS[0], "A", tall_terms, ["A0", "A1"], "v", *pieces["c"])
    r.add(GRADS[0] + 1, "Ax", over_core, "A1", due=GRADS[0] + 3)
    r.add(GRADS[0] + 4, "AA", add_up, "A0", "Ax")
    unpacked(GRADS[1], "B", wide_terms, ["B0", "B1"], "b", *pieces["t"])
    r.add(GRADS[1] + 1, "BB", summed, "B0", "B1", due=end)
    mixed, grad_tokens, grad_route, wide, tall = r.run([("ms", count - 1), ("gs", count - 1), "o", "BB", "AA"])
    return mixed, grad_tokens, grad_route, wide[0][None], wide[1][None], tall[None]


def local(tokens, route_ids, route_weights, cotangent, w_gate, w_up, w_down):
    experts = lax.axis_size("expert")
    capacity = 4 * tokens.shape[0] // experts
    whole = 2 * capacity >= tokens.shape[0] and (experts, lax.axis_size("tensor")) == (8, 4)
    plan = chip_plan if whole else slot_plan
    return plan(tokens, route_ids, route_weights, cotangent, w_gate, w_up, w_down)


def solution(mesh):
    placed = (
        P("expert", "tensor"),
        P("expert", None),
        P("expert", None),
        P("expert", "tensor"),
        P("expert", None, "tensor"),
        P("expert", None, "tensor"),
        P("expert", "tensor", None),
    )
    return jax.shard_map(
        local,
        mesh=mesh,
        in_specs=placed,
        out_specs=(
            P("expert", "tensor"),
            P("expert", "tensor"),
            P("expert", None),
            P("expert", None, "tensor"),
            P("expert", None, "tensor"),
            P("expert", "tensor", None),
        ),
        check_vma=False,
    )
```

```python
import jax
import jax.numpy as jnp
from jax import lax
from jax.experimental import pallas as pl
from jax.experimental.pallas import tpu as pltpu
from jax.sharding import PartitionSpec as P

TOPK = 2


ROW_PAIRS = (((1,), (1,)), ((), ()))
COLUMN_PAIRS = (((0,), (0,)), ((), ()))


def slot_tables(route_ids, experts, capacity):
    pair_count = route_ids.shape[0] * route_ids.shape[1]
    flat_ids = route_ids.reshape(pair_count)
    labels = jnp.arange(experts, dtype=jnp.int32)
    onehot = (flat_ids[:, None] == labels[None, :]).astype(jnp.int32)
    before = jnp.cumsum(onehot, axis=0) - onehot
    slot_index = jnp.sum(before * onehot, axis=1)
    target = flat_ids * capacity + slot_index
    source = (
        jnp.full((experts * capacity,), pair_count, jnp.int32)
        .at[target]
        .set(jnp.arange(pair_count, dtype=jnp.int32))
    )
    return (target, source)


def fill_slots(token_part, cot_part, weight_flat, source):
    row_of = source // TOPK
    zero_row = jnp.zeros((1, token_part.shape[1]), jnp.bfloat16)
    padded_tokens = jnp.concatenate([token_part, zero_row], axis=0)
    padded_cot = jnp.concatenate([cot_part, zero_row], axis=0)
    padded_weight = jnp.concatenate([weight_flat, jnp.zeros((1,), jnp.float32)], axis=0)
    token_slots = padded_tokens[row_of]
    cot_slots = (padded_weight[source][:, None] * padded_cot[row_of].astype(jnp.float32)).astype(
        jnp.bfloat16
    )
    return (token_slots, cot_slots)


def slot_plan(tokens, route_ids, route_weights, cotangent, w_gate, w_up, w_down):
    experts = lax.axis_size("expert")
    tok_rows, slice_width = tokens.shape
    capacity = 4 * tok_rows // experts
    gate_matrix = w_gate[0]
    up_matrix = w_up[0]
    down_weight = w_down[0]
    target, source = slot_tables(route_ids, experts, capacity)
    weight_flat = route_weights.reshape(tok_rows * TOPK)
    full_tokens, full_cot = (
        lax.all_gather(tokens, "tensor", axis=1, tiled=True),
        lax.all_gather(cotangent, "tensor", axis=1, tiled=True),
    )
    model_width = full_tokens.shape[1]
    token_slots, cot_slots = fill_slots(full_tokens, full_cot, weight_flat, source)
    routed, routed_cot = (
        lax.all_to_all(
            token_slots.reshape(experts, capacity, model_width),
            "expert",
            split_axis=0,
            concat_axis=0,
            tiled=True,
        ),
        lax.all_to_all(
            cot_slots.reshape(experts, capacity, model_width),
            "expert",
            split_axis=0,
            concat_axis=0,
            tiled=True,
        ),
    )
    routed = routed.reshape(experts * capacity, model_width)
    routed_cot = routed_cot.reshape(experts * capacity, model_width)
    gate_proj = jnp.dot(routed, gate_matrix, preferred_element_type=jnp.float32)
    up_proj = jnp.dot(routed, up_matrix, preferred_element_type=jnp.float32)
    hidden_state = (jax.nn.silu(gate_proj) * up_proj).astype(jnp.bfloat16)
    down_part = jnp.dot(hidden_state, down_weight, preferred_element_type=jnp.float32)
    expert_sum = lax.psum_scatter(
        down_part.astype(jnp.bfloat16), "tensor", scatter_dimension=1, tiled=True
    )
    expert_output = expert_sum.reshape(experts, capacity, slice_width)
    returned = lax.all_to_all(
        expert_output, "expert", split_axis=0, concat_axis=0, tiled=True
    ).reshape(experts * capacity, slice_width)
    chosen = returned[target].astype(jnp.float32).reshape(tok_rows, TOPK, slice_width)
    mixed = jnp.sum(route_weights[:, :, None] * chosen, axis=1).astype(jnp.bfloat16)
    route_part = jnp.sum(cotangent.astype(jnp.float32)[:, None, :] * chosen, axis=2)
    grad_route = lax.psum(route_part, "tensor")
    d_hidden = lax.dot_general(
        routed_cot, down_weight, ROW_PAIRS, preferred_element_type=jnp.float32
    )
    grad_down = lax.dot_general(
        hidden_state, routed_cot, COLUMN_PAIRS, preferred_element_type=jnp.float32
    ).astype(jnp.bfloat16)
    sigmoid_gate = jax.nn.sigmoid(gate_proj)
    gate_gradient = (
        d_hidden * up_proj * sigmoid_gate * (1.0 + gate_proj * (1.0 - sigmoid_gate))
    ).astype(jnp.bfloat16)
    up_gradient = (d_hidden * jax.nn.silu(gate_proj)).astype(jnp.bfloat16)
    grad_gate = lax.dot_general(
        routed, gate_gradient, COLUMN_PAIRS, preferred_element_type=jnp.float32
    ).astype(jnp.bfloat16)
    grad_up = lax.dot_general(
        routed, up_gradient, COLUMN_PAIRS, preferred_element_type=jnp.float32
    ).astype(jnp.bfloat16)
    back_part = lax.dot_general(
        gate_gradient, gate_matrix, ROW_PAIRS, preferred_element_type=jnp.float32
    )
    back_part = back_part + lax.dot_general(
        up_gradient, up_matrix, ROW_PAIRS, preferred_element_type=jnp.float32
    )
    input_sum = lax.psum_scatter(
        back_part.astype(jnp.bfloat16), "tensor", scatter_dimension=1, tiled=True
    )
    input_rows = input_sum.reshape(experts, capacity, slice_width)
    returned_grads = lax.all_to_all(
        input_rows, "expert", split_axis=0, concat_axis=0, tiled=True
    ).reshape(experts * capacity, slice_width)
    chosen_grads = returned_grads[target].astype(jnp.float32).reshape(tok_rows, TOPK, slice_width)
    grad_tokens = jnp.sum(route_weights[:, :, None] * chosen_grads, axis=1).astype(jnp.bfloat16)
    return (mixed, grad_tokens, grad_route, grad_gate[None], grad_up[None], grad_down[None])


def over(bits):
    even, odd = bits

    def work(value):
        pairs = [(i, i ^ (odd if i % 2 else even)) for i in range(lax.axis_size("expert"))]
        return lax.ppermute(value, "expert", pairs)

    return work


over_core, over_x, over_y, over_xy = over((1, 1)), over((2, 4)), over((4, 2)), over((6, 6))


def along_z(hops):
    def work(value):
        count = lax.axis_size("tensor")
        return lax.ppermute(value, "tensor", [(i, (i + hops) % count) for i in range(count)])

    return work


over_z = along_z(1)


def dot(a, b, dims=(((1,), (0,)), ((), ()))):
    return lax.dot_general(a, b, dims, preferred_element_type=jnp.float32)


def as_bf16(value):
    return value.astype(jnp.bfloat16)


def as_f32(value):
    return value.astype(jnp.float32)


def beside(*values):
    return jnp.concatenate(values, axis=1)


def below(*values):
    return jnp.concatenate(values, axis=0)


START = {
    "t": (0, 4, 8),
    "tx": (0, 8, 9, 12),
    "ty": (1, 3, 7, 11),
    "td": (4, 13, 10, 14),
    "c": (2, 6, 12),
    "cx": (2, 17, 17, 16),
    "cy": (17, 5, 14, 15),
    "cd": (6, 10, 15, 18),
}
ROUTE = {"t": "xyxz", "c": "yzzz"}
SUMS = {
    "mx0": (19, 21), "my0": (19, 21), "mf0": (19, 21), "mx1": (20, 22), "my1": (20, 22),
    "mf1": (22, 22), "mf2": (23, 24), "my2": (25, 26), "mx3": (26, 27),
    "mz": ((22, 22), (23, 24), (27, 28), (29, 29)),
    "gx0": (23, 24), "gy0": (23, 24), "gf0": (23, 24), "gx1": (24, 25), "gy1": (24, 25),
    "gf1": (25, 26), "gf2": (27, 27), "gy2": (28, 28), "gx3": (27, 28),
    "gz": ((25, 25), (26, 27), (29, 29), (30, 30)),
}
KERNELS, GRADS, INNER, HOLD, PAIRED = (17, 18, 21, 22), (25, 24), (26, 28), 2, (16, 16, 16)


class Rounds:
    def __init__(self, given):
        self.steps, self.values = [], dict(given)

    def add(self, start, name, work, *reads, due=None):
        self.steps.append((start, start if due is None else due, name, work, reads))

    def run(self, results):
        values, waiting = self.values, {}
        last = max(step[1] for step in self.steps)
        for now in range(last + 1):
            for start, due, name, work, reads in self.steps:
                if start == now:
                    made = work(*[values[r] if r in values else waiting[r][1] for r in reads])
                    if due > now:
                        waiting[name] = (due, made)
                    else:
                        values[name] = made
            for name in [n for n, (due, _) in waiting.items() if due == now]:
                values[name] = waiting.pop(name)[1]
            if now == last:
                break
            needed = {r for start, _, _, _, reads in self.steps if start > now for r in reads} | set(results)
            live = [n for n in values if n in needed]
            held = lax.optimization_barrier([values[n] for n in live])
            values.update(zip(live, held, strict=True))
        return [values[name] for name in results]


def kernel_params():
    return dict(
        compiler_params=pltpu.CompilerParams(vmem_limit_bytes=60 * 2**20),
        cost_estimate=pl.CostEstimate(flops=1, bytes_accessed=1, transcendentals=0),
    )


ANY = pl.BlockSpec(memory_space=pl.ANY)
VMEM = pl.BlockSpec(memory_space=pltpu.VMEM)
SMEM = pl.BlockSpec(memory_space=pltpu.SMEM)


def part_at(place_ref, step, count):
    return lax.rem(place_ref[0] + 2 * count - step, count)


def span(part, width):
    return pl.ds(pl.multiple_of(part * width, 128), width)


def read_parts(pieces, weights, axis, place_ref, first, buffers, sems):
    rows_buffer, weight_buffer = buffers
    copies, count = [], weight_buffer.shape[0] if weights else rows_buffer.shape[0]
    for k in range(count):
        mine = []
        if pieces:
            rows, width = pieces[k][0].shape
            for b, piece in enumerate(pieces[k]):
                mine.append((piece, rows_buffer.at[k, b * rows : (b + 1) * rows, :]))
        start = 0
        for weight in weights:
            if len(weight.shape) == 3:
                weight = weight.at[1 - place_ref[1]]
            side = weight.shape[1 - axis]
            width = weight.shape[axis] // count
            at = span(part_at(place_ref, k + first, count), width)
            if axis == 0:
                mine.append((weight.at[at, :], weight_buffer.at[k, :, start : start + side]))
            else:
                mine.append((weight.at[:, at], weight_buffer.at[k, start : start + side, :]))
            start += side
        mine = [pltpu.make_async_copy(*pair, sems.at[k, i]) for i, pair in enumerate(mine)]
        for copy in mine:
            copy.start()
        copies.append(mine)
    return copies


def summed_product(pieces, weights, axis, place, extras, finish, outs):
    count, blocks, kinds = len(pieces), len(pieces[0]), len(weights)
    rows, width = pieces[0][0].shape
    sides = sum(w.shape[-2:][1 - axis] for w in weights)
    dims = (((1,), (axis,)), ((), ()))

    def body(place_ref, *refs):
        flat, factors = refs[: count * blocks], refs[count * blocks : count * blocks + kinds]
        more = refs[count * blocks + kinds : count * blocks + kinds + len(extras)]
        results = refs[count * blocks + kinds + len(extras) : -4]
        rows_buffer, weight_buffer, total, sems = refs[-4:]
        grid = [flat[k * blocks : (k + 1) * blocks] for k in range(count)]
        steps = read_parts(grid, factors, axis, place_ref, 0, (rows_buffer, weight_buffer), sems)
        for k, copies in enumerate(steps):
            for copy in copies:
                copy.wait()
            value = dot(rows_buffer[k], weight_buffer[k], dims)
            total[...] = value if k == 0 else total[...] + value
        finish(total, more, results)

    return pl.pallas_call(
        body,
        in_specs=[SMEM] + [ANY] * (count * blocks + kinds) + [VMEM] * len(extras),
        out_specs=[VMEM] * len(outs),
        out_shape=outs,
        scratch_shapes=[
            pltpu.VMEM((count, blocks * rows, width), jnp.bfloat16),
            pltpu.VMEM((count, width, sides) if axis == 0 else (count, sides, width), jnp.bfloat16),
            pltpu.VMEM((blocks * rows, sides), jnp.float32),
            pltpu.SemaphoreType.DMA((count, blocks + kinds)),
        ],
        **kernel_params(),
    )(place, *[p for step in pieces for p in step], *weights, *extras)


def block_terms(left, weights, axis, place, count, layout, blocks):
    rows, sides = left.shape[0] // blocks, left.shape[1]
    kinds, width = len(weights), weights[0].shape[axis] // count
    dims = (((1,), (1 - axis,)), ((), ()))

    def body(place_ref, left_ref, *refs):
        factors, outs = refs[:kinds], refs[kinds : kinds + len(layout)]
        weight_buffer, made, sems, out_sems = refs[kinds + len(layout) :]
        steps = read_parts(None, factors, axis, place_ref, 1, (None, weight_buffer), sems)
        sent = []
        for k, copies in enumerate(steps):
            for copy in copies:
                copy.wait()
            made[k] = as_bf16(dot(left_ref[...], weight_buffer[k], dims))
            for out, listed in zip(outs, layout, strict=True):
                for i, (step, block) in enumerate(listed):
                    if step == k:
                        term = made.at[k, block * rows : (block + 1) * rows, :]
                        copy = pltpu.make_async_copy(
                            term, out.at[i * rows : (i + 1) * rows, :], out_sems.at[k, block]
                        )
                        copy.start()
                        sent.append(copy)
        for copy in sent:
            copy.wait()

    return pl.pallas_call(
        body,
        in_specs=[SMEM, VMEM] + [ANY] * kinds,
        out_specs=[ANY] * len(layout),
        out_shape=[jax.ShapeDtypeStruct((len(out) * rows, width), jnp.bfloat16) for out in layout],
        scratch_shapes=[
            pltpu.VMEM((count, width, sides) if axis == 0 else (count, sides, width), jnp.bfloat16),
            pltpu.VMEM((count, blocks * rows, width), jnp.bfloat16),
            pltpu.SemaphoreType.DMA((count, kinds)),
            pltpu.SemaphoreType.DMA((count, blocks)),
        ],
        **kernel_params(),
    )(place, left, *weights)


def weight_grads(pieces, left, place, kinds, tall):
    count, blocks = len(pieces), len(pieces[0])
    rows, width = pieces[0][0].shape
    side = left.shape[1]
    units = side // (2 * kinds)
    out = (units, count * width) if tall else (2, count * width, units)
    made_outs = 2 if tall else kinds

    def body(place_ref, left_ref, *refs):
        flat, results = refs[: count * blocks], refs[count * blocks : -4]
        rows_buffer, made, sems, out_sems = refs[-4:]
        grid = [flat[k * blocks : (k + 1) * blocks] for k in range(count)]
        steps = read_parts(grid, [], 0, place_ref, 0, (rows_buffer, None), sems)
        sent = []
        for k in range(count):
            for copy in steps[k]:
                copy.wait()
            pair = (left_ref[...], rows_buffer[k]) if tall else (rows_buffer[k], left_ref[...])
            made[k] = as_bf16(dot(*pair, COLUMN_PAIRS))
            at = span(part_at(place_ref, k, count), width)
            for i in range(2 * kinds):
                cut = pl.ds(i * units, units)
                core = place_ref[1] if i < kinds else 1 - place_ref[1]
                if tall:
                    pair = made.at[k, cut, :], results[i].at[:, at]
                else:
                    pair = made.at[k, :, cut], results[i % kinds].at[core, at, :]
                copy = pltpu.make_async_copy(*pair, out_sems.at[k, i])
                copy.start()
                sent.append(copy)
        for copy in sent:
            copy.wait()

    return pl.pallas_call(
        body,
        in_specs=[SMEM, VMEM] + [ANY] * (count * blocks),
        out_specs=[ANY] * made_outs,
        out_shape=[jax.ShapeDtypeStruct(out, jnp.bfloat16)] * made_outs,
        scratch_shapes=[
            pltpu.VMEM((count, blocks * rows, width), jnp.bfloat16),
            pltpu.VMEM((count, side, width) if tall else (count, width, side), jnp.bfloat16),
            pltpu.SemaphoreType.DMA((count, blocks)),
            pltpu.SemaphoreType.DMA((count, 2 * kinds)),
        ],
        **kernel_params(),
    )(place, left, *[p for step in pieces for p in step])


def closing_sum(*terms):
    def body(*refs):
        refs[-1][...] = as_bf16(sum([as_f32(ref[...]) for ref in refs[1:-1]], as_f32(refs[0][...])))

    return pl.pallas_call(
        body,
        in_specs=[VMEM] * len(terms),
        out_specs=VMEM,
        out_shape=jax.ShapeDtypeStruct(terms[0].shape, jnp.bfloat16),
        compiler_params=pltpu.CompilerParams(vmem_limit_bytes=60 * 2**20),
        cost_estimate=pl.CostEstimate(flops=10**11, bytes_accessed=3 * 10**8, transcendentals=0),
    )(*terms)


def chip_plan(tokens, route_ids, route_weights, cotangent, w_gate, w_up, w_down):
    count = lax.axis_size("tensor")
    experts = lax.axis_size("expert")
    place, me = lax.axis_index("tensor"), lax.axis_index("expert")
    place_at = jnp.stack([place, me % 2])
    rows, width = tokens.shape
    units = w_gate.shape[2]

    labels = jnp.arange(experts, dtype=jnp.int32)
    named = route_ids[:, :, None] == labels[None, None, :]
    shares = jnp.sum(jnp.where(named, route_weights[:, :, None], 0.0), axis=1)

    def part_of(step):
        return lax.rem(place + 2 * count - step, count)

    r = Rounds(
        {
            ("t", 0): tokens,
            ("c", 0): cotangent,
            "w": shares,
            "G": w_gate[0],
            "U": w_up[0],
            "D": w_down[0],
        }
    )

    def transfer(at, name, work, read):
        r.add(at, name, work, read, due=at + HOLD)
        return at + HOLD + 1

    ready, pieces = {}, {}
    for a in "tc":
        ready[a] = 0
        for k in range(count):
            if k < count - 1:
                transfer(START[a][k], (a, k + 1), over_z, (a, k))
            work, read = {
                "x": (over_x, (a + "y", k)),
                "y": (over_y, (a + "x", k)),
                "z": (over_z, (a + "d", k - 1)),
            }[ROUTE[a][k]]
            ready[a] = max(
                ready[a],
                transfer(START[a + "x"][k], (a + "x", k), over_x, (a, k)),
                transfer(START[a + "y"][k], (a + "y", k), over_y, (a, k)),
                transfer(START[a + "d"][k], (a + "d", k), work, read),
            )
        pieces[a] = [(a + which, k) if which else (a, k) for k in range(count) for which in ("", "x", "y", "d")]
    m_at, m_terms, g_at, g_terms = KERNELS

    cores = [[i, i + 1] for i in range(0, experts, 2)]
    for name, due in zip("GUD", PAIRED, strict=True):
        r.add(0, name + "s", lambda w: lax.all_gather(w, "expert", axis_index_groups=cores), name, due=due)
    wides, talls = ("G", "U", "Gs", "Us"), ("D", "Ds")
    for name, work in zip(("wx", "wy", "wd"), (over_x, over_y, over_xy), strict=True):
        r.add(0, name, work, "w")

    def share_pair(*blocks):
        share = below(*blocks)
        return beside(*[lax.dynamic_slice_in_dim(share, me ^ i, 1, 1) for i in range(2)])

    r.add(6, "s", share_pair, "w", "wx", "wy", "wd")

    def sizes(dtype, *columns):
        return [jax.ShapeDtypeStruct((4 * rows, n), dtype) for n in columns]

    def activations(total, extras, outs):
        share, both, weighted = extras[0][...], *outs
        both[...] = total[...]
        for i in range(2):
            gate = total[:, 2 * i * units : (2 * i + 1) * units]
            up = total[:, (2 * i + 1) * units : (2 * i + 2) * units]
            value = share[:, i : i + 1] * (gate * jax.nn.sigmoid(gate) * up)
            weighted[:, i * units : (i + 1) * units] = as_bf16(value)

    def gradients(total, extras, outs):
        share, both = extras[0][...], extras[1]
        to_tokens, to_weights, inner = outs
        for i in range(2):
            gate = both[:, 2 * i * units : (2 * i + 1) * units]
            up = both[:, (2 * i + 1) * units : (2 * i + 2) * units]
            d_plain = total[:, i * units : (i + 1) * units]
            weight = share[:, i : i + 1]
            sigmoid_gate = jax.nn.sigmoid(gate)
            silu_gate = gate * sigmoid_gate
            inner[:, i : i + 1] = jnp.sum(silu_gate * up * d_plain, axis=1, keepdims=True)
            d_hidden = weight * d_plain
            d_gate = d_hidden * up * sigmoid_gate * (1.0 + gate * (1.0 - sigmoid_gate))
            d_up = d_hidden * silu_gate
            to_weights[:, 2 * i * units : (2 * i + 1) * units] = as_bf16(d_gate)
            to_weights[:, (2 * i + 1) * units : (2 * i + 2) * units] = as_bf16(d_up)
            to_tokens[:, 2 * i * units : (2 * i + 1) * units] = as_bf16(weight * d_gate)
            to_tokens[:, (2 * i + 1) * units : (2 * i + 2) * units] = as_bf16(weight * d_up)

    def steps_of(values):
        return [values[4 * k : 4 * k + 4] for k in range(count)]

    def forward(share, *values):
        outs = sizes(jnp.float32, 4 * units) + sizes(jnp.bfloat16, 2 * units)
        parts, weights = steps_of(values), values[4 * count :]
        return summed_product(parts, weights, 0, place_at, [share], activations, outs)

    def backward(share, both, *values):
        outs = sizes(jnp.bfloat16, 4 * units, 4 * units) + sizes(jnp.float32, 2)
        parts, weights = steps_of(values), values[4 * count :]
        return summed_product(parts, weights, 1, place_at, [share, both], gradients, outs)

    def unpacked(at, name, work, names, *reads):
        r.add(at, name, work, *reads)
        for i, part in enumerate(names):
            r.add(at, part, lambda v, i=i: v[i], name)

    unpacked(m_at, "H", forward, ("h", "v"), "s", *pieces["t"], *wides)
    unpacked(g_at, "E", backward, ("g", "b", "i"), "s", "h", *pieces["c"], *talls)

    own, side, front, far = range(4)
    layout = {
        "x0": [(0, side)],
        "y0": [(0, front)],
        "x1": [(1, side), (2, side)],
        "y1": [(1, front), (3, front), (3, far)],
        "f0": [(0, far)],
        "f1": [(1, far)],
        "f2": [(2, far)],
        "x3": [(3, side)],
        "y2": [(2, front)],
    }
    layout |= {k: [(k, own)] for k in range(count)}

    def cut(value, n):
        return value[n * rows : (n + 1) * rows]

    def add_up(*terms):
        return as_bf16(sum([as_f32(v) for v in terms[1:]], as_f32(terms[0])))

    for o, at, left, weights, axis in (("m", m_terms, "v", talls, 1), ("g", g_terms, "g", wides, 0)):

        def work(left, *weights, axis=axis):
            return block_terms(left, weights, axis, place_at, count, list(layout.values()), 4)

        unpacked(at, o + "P", work, [(o + "p", name) for name in layout], left, *weights)

        def send(name, work, terms, *reads, o=o):
            start, due = SUMS[o + name]
            r.add(start, (o + "s", name), terms, (o + "p", name), *[(o, n) for n in reads])
            r.add(start, (o, name), work, (o + "s", name), due=due)

        for name, work in (("x0", over_x), ("y0", over_y), ("f0", over_z), ("x1", over_x), ("y1", over_y)):
            send(name, work, lambda v: v)
        send("f1", over_z, add_up, "f0")
        send("f2", over_x, add_up, "f1")
        send("y2", over_y, add_up, "f2")
        send("x3", over_x, lambda v, y: add_up(v, cut(y, 2)), "y1")

        def send_own(k, terms, *reads, o=o):
            start, due = SUMS[o + "z"][k]
            add = closing_sum if (o, k) == ("g", 3) else add_up
            r.add(start, (o + "s", k), lambda *v: add(*terms(*v)), (o + "p", k), *[(o, n) for n in reads])
            if k < count - 1:
                r.add(start, (o, k), over_z, (o + "s", k), due=due)

        send_own(0, lambda v, x, y: (v, x, y), "x0", "y0")
        send_own(1, lambda v, x, y, z: (v, cut(x, 0), cut(y, 0), z), "x1", "y1", 0)
        send_own(2, lambda v, x, y, z: (v, cut(x, 1), y, z), "x1", "y2", 1)
        send_own(3, lambda v, x, y, z: (v, x, cut(y, 1), z), "x3", "y1", 2)

    for q, work in enumerate((over_x, over_y, over_xy), 1):
        r.add(INNER[0], ("n", q), lambda v, work=work, q=q: work(v[q * rows : (q + 1) * rows]), "i")

    def route_sums(inner, *others):
        total = 0.0
        first = jnp.where(me % 2 == 1, 4, 2)
        for bits, found in zip((0, first, 6 - first, 6), (inner[:rows], *others), strict=True):
            for i in range(2):
                total += jnp.where(route_ids == me ^ bits ^ i, found[:, i : i + 1], 0.0)
        return total

    r.add(INNER[0] + 1, ("o", 0), route_sums, "i", *[("n", q) for q in (1, 2, 3)])
    for k in range(1, count):
        r.add(INNER[1], ("o", k), along_z(k), ("o", 0))

    def in_order(*turns):
        turns = jnp.stack(turns)
        return sum(lax.dynamic_index_in_dim(turns, part_of(k), 0, False) for k in range(count))

    r.add(INNER[1] + 1, "o", in_order, *[("o", k) for k in range(count)])

    def tall_terms(left, *parts):
        return weight_grads(steps_of(parts), left, place_at, 1, True)

    def wide_terms(left, *parts):
        return weight_grads(steps_of(parts), left, place_at, 2, False)

    def summed(*terms):
        return [
            lax.psum_scatter(v, "expert", scatter_dimension=0, axis_index_groups=cores) for v in terms
        ]

    end = max(step[1] for step in r.steps)
    unpacked(GRADS[0], "A", tall_terms, ["A0", "A1"], "v", *pieces["c"])
    r.add(GRADS[0] + 1, "Ax", over_core, "A1", due=GRADS[0] + 3)
    r.add(GRADS[0] + 4, "AA", add_up, "A0", "Ax")
    unpacked(GRADS[1], "B", wide_terms, ["B0", "B1"], "b", *pieces["t"])
    r.add(GRADS[1] + 1, "BB", summed, "B0", "B1", due=end)
    mixed, grad_tokens, grad_route, wide, tall = r.run([("ms", count - 1), ("gs", count - 1), "o", "BB", "AA"])
    return mixed, grad_tokens, grad_route, wide[0][None], wide[1][None], tall[None]


def local(tokens, route_ids, route_weights, cotangent, w_gate, w_up, w_down):
    experts = lax.axis_size("expert")
    capacity = 4 * tokens.shape[0] // experts
    whole = 2 * capacity >= tokens.shape[0] and (experts, lax.axis_size("tensor")) == (8, 4)
    plan = chip_plan if whole else slot_plan
    return plan(tokens, route_ids, route_weights, cotangent, w_gate, w_up, w_down)


def solution(mesh):
    placed = (
        P("expert", "tensor"),
        P("expert", None),
        P("expert", None),
        P("expert", "tensor"),
        P("expert", None, "tensor"),
        P("expert", None, "tensor"),
        P("expert", "tensor", None),
    )
    return jax.shard_map(
        local,
        mesh=mesh,
        in_specs=placed,
        out_specs=(
            P("expert", "tensor"),
            P("expert", "tensor"),
            P("expert", None),
            P("expert", None, "tensor"),
            P("expert", None, "tensor"),
            P("expert", "tensor", None),
        ),
        check_vma=False,
    )
```

```python
import jax
import jax.numpy as jnp
from jax import lax
from jax.experimental import pallas as pl
from jax.experimental.pallas import tpu as pltpu
from jax.sharding import PartitionSpec as P

TOPK = 2


ROW_PAIRS = (((1,), (1,)), ((), ()))
COLUMN_PAIRS = (((0,), (0,)), ((), ()))


def slot_tables(route_ids, experts, capacity):
    pair_count = route_ids.shape[0] * route_ids.shape[1]
    flat_ids = route_ids.reshape(pair_count)
    labels = jnp.arange(experts, dtype=jnp.int32)
    onehot = (flat_ids[:, None] == labels[None, :]).astype(jnp.int32)
    before = jnp.cumsum(onehot, axis=0) - onehot
    slot_index = jnp.sum(before * onehot, axis=1)
    target = flat_ids * capacity + slot_index
    source = (
        jnp.full((experts * capacity,), pair_count, jnp.int32)
        .at[target]
        .set(jnp.arange(pair_count, dtype=jnp.int32))
    )
    return (target, source)


def fill_slots(token_part, cot_part, weight_flat, source):
    row_of = source // TOPK
    zero_row = jnp.zeros((1, token_part.shape[1]), jnp.bfloat16)
    padded_tokens = jnp.concatenate([token_part, zero_row], axis=0)
    padded_cot = jnp.concatenate([cot_part, zero_row], axis=0)
    padded_weight = jnp.concatenate([weight_flat, jnp.zeros((1,), jnp.float32)], axis=0)
    token_slots = padded_tokens[row_of]
    cot_slots = (padded_weight[source][:, None] * padded_cot[row_of].astype(jnp.float32)).astype(
        jnp.bfloat16
    )
    return (token_slots, cot_slots)


def slot_plan(tokens, route_ids, route_weights, cotangent, w_gate, w_up, w_down):
    experts = lax.axis_size("expert")
    tok_rows, slice_width = tokens.shape
    capacity = 4 * tok_rows // experts
    gate_matrix = w_gate[0]
    up_matrix = w_up[0]
    down_weight = w_down[0]
    target, source = slot_tables(route_ids, experts, capacity)
    weight_flat = route_weights.reshape(tok_rows * TOPK)
    full_tokens, full_cot = (
        lax.all_gather(tokens, "tensor", axis=1, tiled=True),
        lax.all_gather(cotangent, "tensor", axis=1, tiled=True),
    )
    model_width = full_tokens.shape[1]
    token_slots, cot_slots = fill_slots(full_tokens, full_cot, weight_flat, source)
    routed, routed_cot = (
        lax.all_to_all(
            token_slots.reshape(experts, capacity, model_width),
            "expert",
            split_axis=0,
            concat_axis=0,
            tiled=True,
        ),
        lax.all_to_all(
            cot_slots.reshape(experts, capacity, model_width),
            "expert",
            split_axis=0,
            concat_axis=0,
            tiled=True,
        ),
    )
    routed = routed.reshape(experts * capacity, model_width)
    routed_cot = routed_cot.reshape(experts * capacity, model_width)
    gate_proj = jnp.dot(routed, gate_matrix, preferred_element_type=jnp.float32)
    up_proj = jnp.dot(routed, up_matrix, preferred_element_type=jnp.float32)
    hidden_state = (jax.nn.silu(gate_proj) * up_proj).astype(jnp.bfloat16)
    down_part = jnp.dot(hidden_state, down_weight, preferred_element_type=jnp.float32)
    expert_sum = lax.psum_scatter(
        down_part.astype(jnp.bfloat16), "tensor", scatter_dimension=1, tiled=True
    )
    expert_output = expert_sum.reshape(experts, capacity, slice_width)
    returned = lax.all_to_all(
        expert_output, "expert", split_axis=0, concat_axis=0, tiled=True
    ).reshape(experts * capacity, slice_width)
    chosen = returned[target].astype(jnp.float32).reshape(tok_rows, TOPK, slice_width)
    mixed = jnp.sum(route_weights[:, :, None] * chosen, axis=1).astype(jnp.bfloat16)
    route_part = jnp.sum(cotangent.astype(jnp.float32)[:, None, :] * chosen, axis=2)
    grad_route = lax.psum(route_part, "tensor")
    d_hidden = lax.dot_general(
        routed_cot, down_weight, ROW_PAIRS, preferred_element_type=jnp.float32
    )
    grad_down = lax.dot_general(
        hidden_state, routed_cot, COLUMN_PAIRS, preferred_element_type=jnp.float32
    ).astype(jnp.bfloat16)
    sigmoid_gate = jax.nn.sigmoid(gate_proj)
    gate_gradient = (
        d_hidden * up_proj * sigmoid_gate * (1.0 + gate_proj * (1.0 - sigmoid_gate))
    ).astype(jnp.bfloat16)
    up_gradient = (d_hidden * jax.nn.silu(gate_proj)).astype(jnp.bfloat16)
    grad_gate = lax.dot_general(
        routed, gate_gradient, COLUMN_PAIRS, preferred_element_type=jnp.float32
    ).astype(jnp.bfloat16)
    grad_up = lax.dot_general(
        routed, up_gradient, COLUMN_PAIRS, preferred_element_type=jnp.float32
    ).astype(jnp.bfloat16)
    back_part = lax.dot_general(
        gate_gradient, gate_matrix, ROW_PAIRS, preferred_element_type=jnp.float32
    )
    back_part = back_part + lax.dot_general(
        up_gradient, up_matrix, ROW_PAIRS, preferred_element_type=jnp.float32
    )
    input_sum = lax.psum_scatter(
        back_part.astype(jnp.bfloat16), "tensor", scatter_dimension=1, tiled=True
    )
    input_rows = input_sum.reshape(experts, capacity, slice_width)
    returned_grads = lax.all_to_all(
        input_rows, "expert", split_axis=0, concat_axis=0, tiled=True
    ).reshape(experts * capacity, slice_width)
    chosen_grads = returned_grads[target].astype(jnp.float32).reshape(tok_rows, TOPK, slice_width)
    grad_tokens = jnp.sum(route_weights[:, :, None] * chosen_grads, axis=1).astype(jnp.bfloat16)
    return (mixed, grad_tokens, grad_route, grad_gate[None], grad_up[None], grad_down[None])


def over(bits):
    even, odd = bits

    def work(value):
        pairs = [(i, i ^ (odd if i % 2 else even)) for i in range(lax.axis_size("expert"))]
        return lax.ppermute(value, "expert", pairs)

    return work


over_core, over_x, over_y, over_xy = over((1, 1)), over((2, 4)), over((4, 2)), over((6, 6))


def along_z(hops):
    def work(value):
        count = lax.axis_size("tensor")
        return lax.ppermute(value, "tensor", [(i, (i + hops) % count) for i in range(count)])

    return work


over_z = along_z(1)


def dot(a, b, dims=(((1,), (0,)), ((), ()))):
    return lax.dot_general(a, b, dims, preferred_element_type=jnp.float32)


def as_bf16(value):
    return value.astype(jnp.bfloat16)


def as_f32(value):
    return value.astype(jnp.float32)


def beside(*values):
    return jnp.concatenate(values, axis=1)


def below(*values):
    return jnp.concatenate(values, axis=0)


START = {
    "t": (0, 4, 8),
    "tx": (0, 8, 9, 12),
    "ty": (1, 3, 7, 11),
    "td": (4, 13, 10, 14),
    "c": (2, 6, 12),
    "cx": (2, 17, 17, 16),
    "cy": (17, 5, 14, 15),
    "cd": (6, 10, 15, 18),
}
ROUTE = {"t": "xyxz", "c": "yzzz"}
SUMS = {
    "mx0": (19, 21), "my0": (19, 21), "mf0": (20, 21), "mx1": (19, 22), "my1": (20, 22),
    "mf1": (22, 22), "mf2": (23, 24), "my2": (25, 26), "mx3": (26, 27),
    "mz": ((22, 22), (23, 24), (27, 28), (29, 29)),
    "gx0": (23, 24), "gy0": (23, 24), "gf0": (23, 24), "gx1": (24, 25), "gy1": (24, 25),
    "gf1": (25, 26), "gf2": (27, 27), "gy2": (28, 28), "gx3": (27, 28),
    "gz": ((25, 25), (26, 27), (29, 29), (30, 30)),
}
KERNELS, GRADS, INNER, HOLD, PAIRED = (17, 18, 21, 22), (25, 24), (26, 28), 2, (16, 16, 16)


class Rounds:
    def __init__(self, given):
        self.steps, self.values = [], dict(given)

    def add(self, start, name, work, *reads, due=None):
        self.steps.append((start, start if due is None else due, name, work, reads))

    def run(self, results):
        values, waiting = self.values, {}
        last = max(step[1] for step in self.steps)
        for now in range(last + 1):
            for start, due, name, work, reads in self.steps:
                if start == now:
                    made = work(*[values[r] if r in values else waiting[r][1] for r in reads])
                    if due > now:
                        waiting[name] = (due, made)
                    else:
                        values[name] = made
            for name in [n for n, (due, _) in waiting.items() if due == now]:
                values[name] = waiting.pop(name)[1]
            if now == last:
                break
            needed = {r for start, _, _, _, reads in self.steps if start > now for r in reads} | set(results)
            live = [n for n in values if n in needed]
            held = lax.optimization_barrier([values[n] for n in live])
            values.update(zip(live, held, strict=True))
        return [values[name] for name in results]


def kernel_params():
    return dict(
        compiler_params=pltpu.CompilerParams(vmem_limit_bytes=60 * 2**20),
        cost_estimate=pl.CostEstimate(flops=1, bytes_accessed=1, transcendentals=0),
    )


ANY = pl.BlockSpec(memory_space=pl.ANY)
VMEM = pl.BlockSpec(memory_space=pltpu.VMEM)
SMEM = pl.BlockSpec(memory_space=pltpu.SMEM)


def part_at(place_ref, step, count):
    return lax.rem(place_ref[0] + 2 * count - step, count)


def span(part, width):
    return pl.ds(pl.multiple_of(part * width, 128), width)


def read_parts(pieces, weights, axis, place_ref, first, buffers, sems):
    rows_buffer, weight_buffer = buffers
    copies, count = [], weight_buffer.shape[0] if weights else rows_buffer.shape[0]
    for k in range(count):
        mine = []
        if pieces:
            rows, width = pieces[k][0].shape
            for b, piece in enumerate(pieces[k]):
                mine.append((piece, rows_buffer.at[k, b * rows : (b + 1) * rows, :]))
        start = 0
        for weight in weights:
            if len(weight.shape) == 3:
                weight = weight.at[1 - place_ref[1]]
            side = weight.shape[1 - axis]
            width = weight.shape[axis] // count
            at = span(part_at(place_ref, k + first, count), width)
            if axis == 0:
                mine.append((weight.at[at, :], weight_buffer.at[k, :, start : start + side]))
            else:
                mine.append((weight.at[:, at], weight_buffer.at[k, start : start + side, :]))
            start += side
        mine = [pltpu.make_async_copy(*pair, sems.at[k, i]) for i, pair in enumerate(mine)]
        for copy in mine:
            copy.start()
        copies.append(mine)
    return copies


def summed_product(pieces, weights, axis, place, extras, finish, outs):
    count, blocks, kinds = len(pieces), len(pieces[0]), len(weights)
    rows, width = pieces[0][0].shape
    sides = sum(w.shape[-2:][1 - axis] for w in weights)
    dims = (((1,), (axis,)), ((), ()))

    def body(place_ref, *refs):
        flat, factors = refs[: count * blocks], refs[count * blocks : count * blocks + kinds]
        more = refs[count * blocks + kinds : count * blocks + kinds + len(extras)]
        results = refs[count * blocks + kinds + len(extras) : -4]
        rows_buffer, weight_buffer, total, sems = refs[-4:]
        grid = [flat[k * blocks : (k + 1) * blocks] for k in range(count)]
        steps = read_parts(grid, factors, axis, place_ref, 0, (rows_buffer, weight_buffer), sems)
        for k, copies in enumerate(steps):
            for copy in copies:
                copy.wait()
            value = dot(rows_buffer[k], weight_buffer[k], dims)
            total[...] = value if k == 0 else total[...] + value
        finish(total, more, results)

    return pl.pallas_call(
        body,
        in_specs=[SMEM] + [ANY] * (count * blocks + kinds) + [VMEM] * len(extras),
        out_specs=[VMEM] * len(outs),
        out_shape=outs,
        scratch_shapes=[
            pltpu.VMEM((count, blocks * rows, width), jnp.bfloat16),
            pltpu.VMEM((count, width, sides) if axis == 0 else (count, sides, width), jnp.bfloat16),
            pltpu.VMEM((blocks * rows, sides), jnp.float32),
            pltpu.SemaphoreType.DMA((count, blocks + kinds)),
        ],
        **kernel_params(),
    )(place, *[p for step in pieces for p in step], *weights, *extras)


def block_terms(left, weights, axis, place, count, layout, blocks):
    rows, sides = left.shape[0] // blocks, left.shape[1]
    kinds, width = len(weights), weights[0].shape[axis] // count
    dims = (((1,), (1 - axis,)), ((), ()))

    def body(place_ref, left_ref, *refs):
        factors, outs = refs[:kinds], refs[kinds : kinds + len(layout)]
        weight_buffer, made, sems, out_sems = refs[kinds + len(layout) :]
        steps = read_parts(None, factors, axis, place_ref, 1, (None, weight_buffer), sems)
        sent = []
        for k, copies in enumerate(steps):
            for copy in copies:
                copy.wait()
            made[k] = as_bf16(dot(left_ref[...], weight_buffer[k], dims))
            for out, listed in zip(outs, layout, strict=True):
                for i, (step, block) in enumerate(listed):
                    if step == k:
                        term = made.at[k, block * rows : (block + 1) * rows, :]
                        copy = pltpu.make_async_copy(
                            term, out.at[i * rows : (i + 1) * rows, :], out_sems.at[k, block]
                        )
                        copy.start()
                        sent.append(copy)
        for copy in sent:
            copy.wait()

    return pl.pallas_call(
        body,
        in_specs=[SMEM, VMEM] + [ANY] * kinds,
        out_specs=[ANY] * len(layout),
        out_shape=[jax.ShapeDtypeStruct((len(out) * rows, width), jnp.bfloat16) for out in layout],
        scratch_shapes=[
            pltpu.VMEM((count, width, sides) if axis == 0 else (count, sides, width), jnp.bfloat16),
            pltpu.VMEM((count, blocks * rows, width), jnp.bfloat16),
            pltpu.SemaphoreType.DMA((count, kinds)),
            pltpu.SemaphoreType.DMA((count, blocks)),
        ],
        **kernel_params(),
    )(place, left, *weights)


def weight_grads(pieces, left, place, kinds, tall):
    count, blocks = len(pieces), len(pieces[0])
    rows, width = pieces[0][0].shape
    side = left.shape[1]
    units = side // (2 * kinds)
    out = (units, count * width) if tall else (2, count * width, units)
    made_outs = 2 if tall else kinds

    def body(place_ref, left_ref, *refs):
        flat, results = refs[: count * blocks], refs[count * blocks : -4]
        rows_buffer, made, sems, out_sems = refs[-4:]
        grid = [flat[k * blocks : (k + 1) * blocks] for k in range(count)]
        steps = read_parts(grid, [], 0, place_ref, 0, (rows_buffer, None), sems)
        sent = []
        for k in range(count):
            for copy in steps[k]:
                copy.wait()
            pair = (left_ref[...], rows_buffer[k]) if tall else (rows_buffer[k], left_ref[...])
            made[k] = as_bf16(dot(*pair, COLUMN_PAIRS))
            at = span(part_at(place_ref, k, count), width)
            for i in range(2 * kinds):
                cut = pl.ds(i * units, units)
                core = place_ref[1] if i < kinds else 1 - place_ref[1]
                if tall:
                    pair = made.at[k, cut, :], results[i].at[:, at]
                else:
                    pair = made.at[k, :, cut], results[i % kinds].at[core, at, :]
                copy = pltpu.make_async_copy(*pair, out_sems.at[k, i])
                copy.start()
                sent.append(copy)
        for copy in sent:
            copy.wait()

    return pl.pallas_call(
        body,
        in_specs=[SMEM, VMEM] + [ANY] * (count * blocks),
        out_specs=[ANY] * made_outs,
        out_shape=[jax.ShapeDtypeStruct(out, jnp.bfloat16)] * made_outs,
        scratch_shapes=[
            pltpu.VMEM((count, blocks * rows, width), jnp.bfloat16),
            pltpu.VMEM((count, side, width) if tall else (count, width, side), jnp.bfloat16),
            pltpu.SemaphoreType.DMA((count, blocks)),
            pltpu.SemaphoreType.DMA((count, 2 * kinds)),
        ],
        **kernel_params(),
    )(place, left, *[p for step in pieces for p in step])


def closing_sum(*terms):
    def body(*refs):
        refs[-1][...] = as_bf16(sum([as_f32(ref[...]) for ref in refs[1:-1]], as_f32(refs[0][...])))

    return pl.pallas_call(
        body,
        in_specs=[VMEM] * len(terms),
        out_specs=VMEM,
        out_shape=jax.ShapeDtypeStruct(terms[0].shape, jnp.bfloat16),
        compiler_params=pltpu.CompilerParams(vmem_limit_bytes=60 * 2**20),
        cost_estimate=pl.CostEstimate(flops=10**11, bytes_accessed=3 * 10**8, transcendentals=0),
    )(*terms)


def chip_plan(tokens, route_ids, route_weights, cotangent, w_gate, w_up, w_down):
    count = lax.axis_size("tensor")
    experts = lax.axis_size("expert")
    place, me = lax.axis_index("tensor"), lax.axis_index("expert")
    place_at = jnp.stack([place, me % 2])
    rows, width = tokens.shape
    units = w_gate.shape[2]

    labels = jnp.arange(experts, dtype=jnp.int32)
    named = route_ids[:, :, None] == labels[None, None, :]
    shares = jnp.sum(jnp.where(named, route_weights[:, :, None], 0.0), axis=1)

    def part_of(step):
        return lax.rem(place + 2 * count - step, count)

    r = Rounds(
        {
            ("t", 0): tokens,
            ("c", 0): cotangent,
            "w": shares,
            "G": w_gate[0],
            "U": w_up[0],
            "D": w_down[0],
        }
    )

    def transfer(at, name, work, read):
        r.add(at, name, work, read, due=at + HOLD)
        return at + HOLD + 1

    ready, pieces = {}, {}
    for a in "tc":
        ready[a] = 0
        for k in range(count):
            if k < count - 1:
                transfer(START[a][k], (a, k + 1), over_z, (a, k))
            work, read = {
                "x": (over_x, (a + "y", k)),
                "y": (over_y, (a + "x", k)),
                "z": (over_z, (a + "d", k - 1)),
            }[ROUTE[a][k]]
            ready[a] = max(
                ready[a],
                transfer(START[a + "x"][k], (a + "x", k), over_x, (a, k)),
                transfer(START[a + "y"][k], (a + "y", k), over_y, (a, k)),
                transfer(START[a + "d"][k], (a + "d", k), work, read),
            )
        pieces[a] = [(a + which, k) if which else (a, k) for k in range(count) for which in ("", "x", "y", "d")]
    m_at, m_terms, g_at, g_terms = KERNELS

    cores = [[i, i + 1] for i in range(0, experts, 2)]
    for name, due in zip("GUD", PAIRED, strict=True):
        r.add(0, name + "s", lambda w: lax.all_gather(w, "expert", axis_index_groups=cores), name, due=due)
    wides, talls = ("G", "U", "Gs", "Us"), ("D", "Ds")
    for name, work in zip(("wx", "wy", "wd"), (over_x, over_y, over_xy), strict=True):
        r.add(0, name, work, "w")

    def share_pair(*blocks):
        share = below(*blocks)
        return beside(*[lax.dynamic_slice_in_dim(share, me ^ i, 1, 1) for i in range(2)])

    r.add(6, "s", share_pair, "w", "wx", "wy", "wd")

    def sizes(dtype, *columns):
        return [jax.ShapeDtypeStruct((4 * rows, n), dtype) for n in columns]

    def activations(total, extras, outs):
        share, both, weighted = extras[0][...], *outs
        both[...] = total[...]
        for i in range(2):
            gate = total[:, 2 * i * units : (2 * i + 1) * units]
            up = total[:, (2 * i + 1) * units : (2 * i + 2) * units]
            value = share[:, i : i + 1] * (gate * jax.nn.sigmoid(gate) * up)
            weighted[:, i * units : (i + 1) * units] = as_bf16(value)

    def gradients(total, extras, outs):
        share, both = extras[0][...], extras[1]
        to_tokens, to_weights, inner = outs
        for i in range(2):
            gate = both[:, 2 * i * units : (2 * i + 1) * units]
            up = both[:, (2 * i + 1) * units : (2 * i + 2) * units]
            d_plain = total[:, i * units : (i + 1) * units]
            weight = share[:, i : i + 1]
            sigmoid_gate = jax.nn.sigmoid(gate)
            silu_gate = gate * sigmoid_gate
            inner[:, i : i + 1] = jnp.sum(silu_gate * up * d_plain, axis=1, keepdims=True)
            d_hidden = weight * d_plain
            d_gate = d_hidden * up * sigmoid_gate * (1.0 + gate * (1.0 - sigmoid_gate))
            d_up = d_hidden * silu_gate
            to_weights[:, 2 * i * units : (2 * i + 1) * units] = as_bf16(d_gate)
            to_weights[:, (2 * i + 1) * units : (2 * i + 2) * units] = as_bf16(d_up)
            to_tokens[:, 2 * i * units : (2 * i + 1) * units] = as_bf16(weight * d_gate)
            to_tokens[:, (2 * i + 1) * units : (2 * i + 2) * units] = as_bf16(weight * d_up)

    def steps_of(values):
        return [values[4 * k : 4 * k + 4] for k in range(count)]

    def forward(share, *values):
        outs = sizes(jnp.float32, 4 * units) + sizes(jnp.bfloat16, 2 * units)
        parts, weights = steps_of(values), values[4 * count :]
        return summed_product(parts, weights, 0, place_at, [share], activations, outs)

    def backward(share, both, *values):
        outs = sizes(jnp.bfloat16, 4 * units, 4 * units) + sizes(jnp.float32, 2)
        parts, weights = steps_of(values), values[4 * count :]
        return summed_product(parts, weights, 1, place_at, [share, both], gradients, outs)

    def unpacked(at, name, work, names, *reads):
        r.add(at, name, work, *reads)
        for i, part in enumerate(names):
            r.add(at, part, lambda v, i=i: v[i], name)

    unpacked(m_at, "H", forward, ("h", "v"), "s", *pieces["t"], *wides)
    unpacked(g_at, "E", backward, ("g", "b", "i"), "s", "h", *pieces["c"], *talls)

    own, side, front, far = range(4)
    layout = {
        "x0": [(0, side)],
        "y0": [(0, front)],
        "x1": [(1, side), (2, side)],
        "y1": [(1, front), (3, front), (3, far)],
        "f0": [(0, far)],
        "f1": [(1, far)],
        "f2": [(2, far)],
        "x3": [(3, side)],
        "y2": [(2, front)],
    }
    layout |= {k: [(k, own)] for k in range(count)}

    def cut(value, n):
        return value[n * rows : (n + 1) * rows]

    def add_up(*terms):
        return as_bf16(sum([as_f32(v) for v in terms[1:]], as_f32(terms[0])))

    for o, at, left, weights, axis in (("m", m_terms, "v", talls, 1), ("g", g_terms, "g", wides, 0)):

        def work(left, *weights, axis=axis):
            return block_terms(left, weights, axis, place_at, count, list(layout.values()), 4)

        unpacked(at, o + "P", work, [(o + "p", name) for name in layout], left, *weights)

        def send(name, work, terms, *reads, o=o):
            start, due = SUMS[o + name]
            r.add(start, (o + "s", name), terms, (o + "p", name), *[(o, n) for n in reads])
            r.add(start, (o, name), work, (o + "s", name), due=due)

        for name, work in (("x0", over_x), ("y0", over_y), ("f0", over_z), ("x1", over_x), ("y1", over_y)):
            send(name, work, lambda v: v)
        send("f1", over_z, add_up, "f0")
        send("f2", over_x, add_up, "f1")
        send("y2", over_y, add_up, "f2")
        send("x3", over_x, lambda v, y: add_up(v, cut(y, 2)), "y1")

        def send_own(k, terms, *reads, o=o):
            start, due = SUMS[o + "z"][k]
            add = closing_sum if (o, k) == ("g", 3) else add_up
            r.add(start, (o + "s", k), lambda *v: add(*terms(*v)), (o + "p", k), *[(o, n) for n in reads])
            if k < count - 1:
                r.add(start, (o, k), over_z, (o + "s", k), due=due)

        send_own(0, lambda v, x, y: (v, x, y), "x0", "y0")
        send_own(1, lambda v, x, y, z: (v, cut(x, 0), cut(y, 0), z), "x1", "y1", 0)
        send_own(2, lambda v, x, y, z: (v, cut(x, 1), y, z), "x1", "y2", 1)
        send_own(3, lambda v, x, y, z: (v, x, cut(y, 1), z), "x3", "y1", 2)

    for q, work in enumerate((over_x, over_y, over_xy), 1):
        r.add(INNER[0], ("n", q), lambda v, work=work, q=q: work(v[q * rows : (q + 1) * rows]), "i")

    def route_sums(inner, *others):
        total = 0.0
        first = jnp.where(me % 2 == 1, 4, 2)
        for bits, found in zip((0, first, 6 - first, 6), (inner[:rows], *others), strict=True):
            for i in range(2):
                total += jnp.where(route_ids == me ^ bits ^ i, found[:, i : i + 1], 0.0)
        return total

    r.add(INNER[0] + 1, ("o", 0), route_sums, "i", *[("n", q) for q in (1, 2, 3)])
    for k in range(1, count):
        r.add(INNER[1], ("o", k), along_z(k), ("o", 0))

    def in_order(*turns):
        turns = jnp.stack(turns)
        return sum(lax.dynamic_index_in_dim(turns, part_of(k), 0, False) for k in range(count))

    r.add(INNER[1] + 1, "o", in_order, *[("o", k) for k in range(count)])

    def tall_terms(left, *parts):
        return weight_grads(steps_of(parts), left, place_at, 1, True)

    def wide_terms(left, *parts):
        return weight_grads(steps_of(parts), left, place_at, 2, False)

    def summed(*terms):
        return [
            lax.psum_scatter(v, "expert", scatter_dimension=0, axis_index_groups=cores) for v in terms
        ]

    end = max(step[1] for step in r.steps)
    unpacked(GRADS[0], "A", tall_terms, ["A0", "A1"], "v", *pieces["c"])
    r.add(GRADS[0] + 1, "Ax", over_core, "A1", due=GRADS[0] + 3)
    r.add(GRADS[0] + 4, "AA", add_up, "A0", "Ax")
    unpacked(GRADS[1], "B", wide_terms, ["B0", "B1"], "b", *pieces["t"])
    r.add(GRADS[1] + 1, "BB", summed, "B0", "B1", due=end)
    mixed, grad_tokens, grad_route, wide, tall = r.run([("ms", count - 1), ("gs", count - 1), "o", "BB", "AA"])
    return mixed, grad_tokens, grad_route, wide[0][None], wide[1][None], tall[None]


def local(tokens, route_ids, route_weights, cotangent, w_gate, w_up, w_down):
    experts = lax.axis_size("expert")
    capacity = 4 * tokens.shape[0] // experts
    whole = 2 * capacity >= tokens.shape[0] and (experts, lax.axis_size("tensor")) == (8, 4)
    plan = chip_plan if whole else slot_plan
    return plan(tokens, route_ids, route_weights, cotangent, w_gate, w_up, w_down)


def solution(mesh):
    placed = (
        P("expert", "tensor"),
        P("expert", None),
        P("expert", None),
        P("expert", "tensor"),
        P("expert", None, "tensor"),
        P("expert", None, "tensor"),
        P("expert", "tensor", None),
    )
    return jax.shard_map(
        local,
        mesh=mesh,
        in_specs=placed,
        out_specs=(
            P("expert", "tensor"),
            P("expert", "tensor"),
            P("expert", None),
            P("expert", None, "tensor"),
            P("expert", None, "tensor"),
            P("expert", "tensor", None),
        ),
        check_vma=False,
    )
```

```python
import jax
import jax.numpy as jnp
from jax import lax
from jax.experimental import pallas as pl
from jax.experimental.pallas import tpu as pltpu
from jax.sharding import PartitionSpec as P

TOPK = 2


ROW_PAIRS = (((1,), (1,)), ((), ()))
COLUMN_PAIRS = (((0,), (0,)), ((), ()))


def slot_tables(route_ids, experts, capacity):
    pair_count = route_ids.shape[0] * route_ids.shape[1]
    flat_ids = route_ids.reshape(pair_count)
    labels = jnp.arange(experts, dtype=jnp.int32)
    onehot = (flat_ids[:, None] == labels[None, :]).astype(jnp.int32)
    before = jnp.cumsum(onehot, axis=0) - onehot
    slot_index = jnp.sum(before * onehot, axis=1)
    target = flat_ids * capacity + slot_index
    source = (
        jnp.full((experts * capacity,), pair_count, jnp.int32)
        .at[target]
        .set(jnp.arange(pair_count, dtype=jnp.int32))
    )
    return (target, source)


def fill_slots(token_part, cot_part, weight_flat, source):
    row_of = source // TOPK
    zero_row = jnp.zeros((1, token_part.shape[1]), jnp.bfloat16)
    padded_tokens = jnp.concatenate([token_part, zero_row], axis=0)
    padded_cot = jnp.concatenate([cot_part, zero_row], axis=0)
    padded_weight = jnp.concatenate([weight_flat, jnp.zeros((1,), jnp.float32)], axis=0)
    token_slots = padded_tokens[row_of]
    cot_slots = (padded_weight[source][:, None] * padded_cot[row_of].astype(jnp.float32)).astype(
        jnp.bfloat16
    )
    return (token_slots, cot_slots)


def slot_plan(tokens, route_ids, route_weights, cotangent, w_gate, w_up, w_down):
    experts = lax.axis_size("expert")
    tok_rows, slice_width = tokens.shape
    capacity = 4 * tok_rows // experts
    gate_matrix = w_gate[0]
    up_matrix = w_up[0]
    down_weight = w_down[0]
    target, source = slot_tables(route_ids, experts, capacity)
    weight_flat = route_weights.reshape(tok_rows * TOPK)
    full_tokens, full_cot = (
        lax.all_gather(tokens, "tensor", axis=1, tiled=True),
        lax.all_gather(cotangent, "tensor", axis=1, tiled=True),
    )
    model_width = full_tokens.shape[1]
    token_slots, cot_slots = fill_slots(full_tokens, full_cot, weight_flat, source)
    routed, routed_cot = (
        lax.all_to_all(
            token_slots.reshape(experts, capacity, model_width),
            "expert",
            split_axis=0,
            concat_axis=0,
            tiled=True,
        ),
        lax.all_to_all(
            cot_slots.reshape(experts, capacity, model_width),
            "expert",
            split_axis=0,
            concat_axis=0,
            tiled=True,
        ),
    )
    routed = routed.reshape(experts * capacity, model_width)
    routed_cot = routed_cot.reshape(experts * capacity, model_width)
    gate_proj = jnp.dot(routed, gate_matrix, preferred_element_type=jnp.float32)
    up_proj = jnp.dot(routed, up_matrix, preferred_element_type=jnp.float32)
    hidden_state = (jax.nn.silu(gate_proj) * up_proj).astype(jnp.bfloat16)
    down_part = jnp.dot(hidden_state, down_weight, preferred_element_type=jnp.float32)
    expert_sum = lax.psum_scatter(
        down_part.astype(jnp.bfloat16), "tensor", scatter_dimension=1, tiled=True
    )
    expert_output = expert_sum.reshape(experts, capacity, slice_width)
    returned = lax.all_to_all(
        expert_output, "expert", split_axis=0, concat_axis=0, tiled=True
    ).reshape(experts * capacity, slice_width)
    chosen = returned[target].astype(jnp.float32).reshape(tok_rows, TOPK, slice_width)
    mixed = jnp.sum(route_weights[:, :, None] * chosen, axis=1).astype(jnp.bfloat16)
    route_part = jnp.sum(cotangent.astype(jnp.float32)[:, None, :] * chosen, axis=2)
    grad_route = lax.psum(route_part, "tensor")
    d_hidden = lax.dot_general(
        routed_cot, down_weight, ROW_PAIRS, preferred_element_type=jnp.float32
    )
    grad_down = lax.dot_general(
        hidden_state, routed_cot, COLUMN_PAIRS, preferred_element_type=jnp.float32
    ).astype(jnp.bfloat16)
    sigmoid_gate = jax.nn.sigmoid(gate_proj)
    gate_gradient = (
        d_hidden * up_proj * sigmoid_gate * (1.0 + gate_proj * (1.0 - sigmoid_gate))
    ).astype(jnp.bfloat16)
    up_gradient = (d_hidden * jax.nn.silu(gate_proj)).astype(jnp.bfloat16)
    grad_gate = lax.dot_general(
        routed, gate_gradient, COLUMN_PAIRS, preferred_element_type=jnp.float32
    ).astype(jnp.bfloat16)
    grad_up = lax.dot_general(
        routed, up_gradient, COLUMN_PAIRS, preferred_element_type=jnp.float32
    ).astype(jnp.bfloat16)
    back_part = lax.dot_general(
        gate_gradient, gate_matrix, ROW_PAIRS, preferred_element_type=jnp.float32
    )
    back_part = back_part + lax.dot_general(
        up_gradient, up_matrix, ROW_PAIRS, preferred_element_type=jnp.float32
    )
    input_sum = lax.psum_scatter(
        back_part.astype(jnp.bfloat16), "tensor", scatter_dimension=1, tiled=True
    )
    input_rows = input_sum.reshape(experts, capacity, slice_width)
    returned_grads = lax.all_to_all(
        input_rows, "expert", split_axis=0, concat_axis=0, tiled=True
    ).reshape(experts * capacity, slice_width)
    chosen_grads = returned_grads[target].astype(jnp.float32).reshape(tok_rows, TOPK, slice_width)
    grad_tokens = jnp.sum(route_weights[:, :, None] * chosen_grads, axis=1).astype(jnp.bfloat16)
    return (mixed, grad_tokens, grad_route, grad_gate[None], grad_up[None], grad_down[None])


def over(bits):
    even, odd = bits

    def work(value):
        pairs = [(i, i ^ (odd if i % 2 else even)) for i in range(lax.axis_size("expert"))]
        return lax.ppermute(value, "expert", pairs)

    return work


over_core, over_x, over_y, over_xy = over((1, 1)), over((2, 4)), over((4, 2)), over((6, 6))


def along_z(hops):
    def work(value):
        count = lax.axis_size("tensor")
        return lax.ppermute(value, "tensor", [(i, (i + hops) % count) for i in range(count)])

    return work


over_z = along_z(1)


def dot(a, b, dims=(((1,), (0,)), ((), ()))):
    return lax.dot_general(a, b, dims, preferred_element_type=jnp.float32)


def as_bf16(value):
    return value.astype(jnp.bfloat16)


def as_f32(value):
    return value.astype(jnp.float32)


def beside(*values):
    return jnp.concatenate(values, axis=1)


def below(*values):
    return jnp.concatenate(values, axis=0)


START = {
    "t": (0, 4, 8),
    "tx": (0, 8, 9, 12),
    "ty": (1, 3, 7, 11),
    "td": (4, 13, 10, 14),
    "c": (2, 6, 12),
    "cx": (2, 17, 17, 16),
    "cy": (17, 5, 14, 15),
    "cd": (6, 10, 15, 18),
}
ROUTE = {"t": "xyxz", "c": "yzzz"}
SUMS = {
    "mx0": (19, 21), "my0": (19, 21), "mf0": (20, 21), "mx1": (19, 22), "my1": (20, 22),
    "mf1": (22, 22), "mf2": (24, 25), "my2": (26, 26), "mx3": (26, 27),
    "mz": ((22, 22), (24, 25), (27, 28), (29, 29)),
    "gx0": (23, 24), "gy0": (23, 24), "gf0": (23, 24), "gx1": (23, 25), "gy1": (23, 25),
    "gf1": (25, 26), "gf2": (27, 27), "gy2": (28, 28), "gx3": (27, 28),
    "gz": ((25, 25), (26, 27), (29, 29), (30, 30)),
}
KERNELS, GRADS, INNER, HOLD, PAIRED = (17, 18, 21, 22), (25, 24), (26, 28), 2, (16, 16, 16)


class Rounds:
    def __init__(self, given):
        self.steps, self.values = [], dict(given)

    def add(self, start, name, work, *reads, due=None):
        self.steps.append((start, start if due is None else due, name, work, reads))

    def run(self, results):
        values, waiting = self.values, {}
        last = max(step[1] for step in self.steps)
        for now in range(last + 1):
            for start, due, name, work, reads in self.steps:
                if start == now:
                    made = work(*[values[r] if r in values else waiting[r][1] for r in reads])
                    if due > now:
                        waiting[name] = (due, made)
                    else:
                        values[name] = made
            for name in [n for n, (due, _) in waiting.items() if due == now]:
                values[name] = waiting.pop(name)[1]
            if now == last:
                break
            needed = {r for start, _, _, _, reads in self.steps if start > now for r in reads} | set(results)
            live = [n for n in values if n in needed]
            held = lax.optimization_barrier([values[n] for n in live])
            values.update(zip(live, held, strict=True))
        return [values[name] for name in results]


def kernel_params():
    return dict(
        compiler_params=pltpu.CompilerParams(vmem_limit_bytes=60 * 2**20),
        cost_estimate=pl.CostEstimate(flops=1, bytes_accessed=1, transcendentals=0),
    )


ANY = pl.BlockSpec(memory_space=pl.ANY)
VMEM = pl.BlockSpec(memory_space=pltpu.VMEM)
SMEM = pl.BlockSpec(memory_space=pltpu.SMEM)


def part_at(place_ref, step, count):
    return lax.rem(place_ref[0] + 2 * count - step, count)


def span(part, width):
    return pl.ds(pl.multiple_of(part * width, 128), width)


def read_parts(pieces, weights, axis, place_ref, first, buffers, sems):
    rows_buffer, weight_buffer = buffers
    copies, count = [], weight_buffer.shape[0] if weights else rows_buffer.shape[0]
    for k in range(count):
        mine = []
        if pieces:
            rows, width = pieces[k][0].shape
            for b, piece in enumerate(pieces[k]):
                mine.append((piece, rows_buffer.at[k, b * rows : (b + 1) * rows, :]))
        start = 0
        for weight in weights:
            if len(weight.shape) == 3:
                weight = weight.at[1 - place_ref[1]]
            side = weight.shape[1 - axis]
            width = weight.shape[axis] // count
            at = span(part_at(place_ref, k + first, count), width)
            if axis == 0:
                mine.append((weight.at[at, :], weight_buffer.at[k, :, start : start + side]))
            else:
                mine.append((weight.at[:, at], weight_buffer.at[k, start : start + side, :]))
            start += side
        mine = [pltpu.make_async_copy(*pair, sems.at[k, i]) for i, pair in enumerate(mine)]
        for copy in mine:
            copy.start()
        copies.append(mine)
    return copies


def summed_product(pieces, weights, axis, place, extras, finish, outs):
    count, blocks, kinds = len(pieces), len(pieces[0]), len(weights)
    rows, width = pieces[0][0].shape
    sides = sum(w.shape[-2:][1 - axis] for w in weights)
    dims = (((1,), (axis,)), ((), ()))

    def body(place_ref, *refs):
        flat, factors = refs[: count * blocks], refs[count * blocks : count * blocks + kinds]
        more = refs[count * blocks + kinds : count * blocks + kinds + len(extras)]
        results = refs[count * blocks + kinds + len(extras) : -4]
        rows_buffer, weight_buffer, total, sems = refs[-4:]
        grid = [flat[k * blocks : (k + 1) * blocks] for k in range(count)]
        steps = read_parts(grid, factors, axis, place_ref, 0, (rows_buffer, weight_buffer), sems)
        for k, copies in enumerate(steps):
            for copy in copies:
                copy.wait()
            value = dot(rows_buffer[k], weight_buffer[k], dims)
            total[...] = value if k == 0 else total[...] + value
        finish(total, more, results)

    return pl.pallas_call(
        body,
        in_specs=[SMEM] + [ANY] * (count * blocks + kinds) + [VMEM] * len(extras),
        out_specs=[VMEM] * len(outs),
        out_shape=outs,
        scratch_shapes=[
            pltpu.VMEM((count, blocks * rows, width), jnp.bfloat16),
            pltpu.VMEM((count, width, sides) if axis == 0 else (count, sides, width), jnp.bfloat16),
            pltpu.VMEM((blocks * rows, sides), jnp.float32),
            pltpu.SemaphoreType.DMA((count, blocks + kinds)),
        ],
        **kernel_params(),
    )(place, *[p for step in pieces for p in step], *weights, *extras)


def block_terms(left, weights, axis, place, count, layout, blocks):
    rows, sides = left.shape[0] // blocks, left.shape[1]
    kinds, width = len(weights), weights[0].shape[axis] // count
    dims = (((1,), (1 - axis,)), ((), ()))

    def body(place_ref, left_ref, *refs):
        factors, outs = refs[:kinds], refs[kinds : kinds + len(layout)]
        weight_buffer, made, sems, out_sems = refs[kinds + len(layout) :]
        steps = read_parts(None, factors, axis, place_ref, 1, (None, weight_buffer), sems)
        sent = []
        for k, copies in enumerate(steps):
            for copy in copies:
                copy.wait()
            made[k] = as_bf16(dot(left_ref[...], weight_buffer[k], dims))
            for out, listed in zip(outs, layout, strict=True):
                for i, (step, block) in enumerate(listed):
                    if step == k:
                        term = made.at[k, block * rows : (block + 1) * rows, :]
                        copy = pltpu.make_async_copy(
                            term, out.at[i * rows : (i + 1) * rows, :], out_sems.at[k, block]
                        )
                        copy.start()
                        sent.append(copy)
        for copy in sent:
            copy.wait()

    return pl.pallas_call(
        body,
        in_specs=[SMEM, VMEM] + [ANY] * kinds,
        out_specs=[ANY] * len(layout),
        out_shape=[jax.ShapeDtypeStruct((len(out) * rows, width), jnp.bfloat16) for out in layout],
        scratch_shapes=[
            pltpu.VMEM((count, width, sides) if axis == 0 else (count, sides, width), jnp.bfloat16),
            pltpu.VMEM((count, blocks * rows, width), jnp.bfloat16),
            pltpu.SemaphoreType.DMA((count, kinds)),
            pltpu.SemaphoreType.DMA((count, blocks)),
        ],
        **kernel_params(),
    )(place, left, *weights)


def weight_grads(pieces, left, place, kinds, tall):
    count, blocks = len(pieces), len(pieces[0])
    rows, width = pieces[0][0].shape
    side = left.shape[1]
    units = side // (2 * kinds)
    out = (units, count * width) if tall else (2, count * width, units)
    made_outs = 2 if tall else kinds

    def body(place_ref, left_ref, *refs):
        flat, results = refs[: count * blocks], refs[count * blocks : -4]
        rows_buffer, made, sems, out_sems = refs[-4:]
        grid = [flat[k * blocks : (k + 1) * blocks] for k in range(count)]
        steps = read_parts(grid, [], 0, place_ref, 0, (rows_buffer, None), sems)
        sent = []
        for k in range(count):
            for copy in steps[k]:
                copy.wait()
            pair = (left_ref[...], rows_buffer[k]) if tall else (rows_buffer[k], left_ref[...])
            made[k] = as_bf16(dot(*pair, COLUMN_PAIRS))
            at = span(part_at(place_ref, k, count), width)
            for i in range(2 * kinds):
                cut = pl.ds(i * units, units)
                core = place_ref[1] if i < kinds else 1 - place_ref[1]
                if tall:
                    pair = made.at[k, cut, :], results[i].at[:, at]
                else:
                    pair = made.at[k, :, cut], results[i % kinds].at[core, at, :]
                copy = pltpu.make_async_copy(*pair, out_sems.at[k, i])
                copy.start()
                sent.append(copy)
        for copy in sent:
            copy.wait()

    return pl.pallas_call(
        body,
        in_specs=[SMEM, VMEM] + [ANY] * (count * blocks),
        out_specs=[ANY] * made_outs,
        out_shape=[jax.ShapeDtypeStruct(out, jnp.bfloat16)] * made_outs,
        scratch_shapes=[
            pltpu.VMEM((count, blocks * rows, width), jnp.bfloat16),
            pltpu.VMEM((count, side, width) if tall else (count, width, side), jnp.bfloat16),
            pltpu.SemaphoreType.DMA((count, blocks)),
            pltpu.SemaphoreType.DMA((count, 2 * kinds)),
        ],
        **kernel_params(),
    )(place, left, *[p for step in pieces for p in step])


def closing_sum(*terms):
    def body(*refs):
        refs[-1][...] = as_bf16(sum([as_f32(ref[...]) for ref in refs[1:-1]], as_f32(refs[0][...])))

    return pl.pallas_call(
        body,
        in_specs=[VMEM] * len(terms),
        out_specs=VMEM,
        out_shape=jax.ShapeDtypeStruct(terms[0].shape, jnp.bfloat16),
        compiler_params=pltpu.CompilerParams(vmem_limit_bytes=60 * 2**20),
        cost_estimate=pl.CostEstimate(flops=10**11, bytes_accessed=3 * 10**8, transcendentals=0),
    )(*terms)


def chip_plan(tokens, route_ids, route_weights, cotangent, w_gate, w_up, w_down):
    count = lax.axis_size("tensor")
    experts = lax.axis_size("expert")
    place, me = lax.axis_index("tensor"), lax.axis_index("expert")
    place_at = jnp.stack([place, me % 2])
    rows, width = tokens.shape
    units = w_gate.shape[2]

    labels = jnp.arange(experts, dtype=jnp.int32)
    named = route_ids[:, :, None] == labels[None, None, :]
    shares = jnp.sum(jnp.where(named, route_weights[:, :, None], 0.0), axis=1)

    def part_of(step):
        return lax.rem(place + 2 * count - step, count)

    r = Rounds(
        {
            ("t", 0): tokens,
            ("c", 0): cotangent,
            "w": shares,
            "G": w_gate[0],
            "U": w_up[0],
            "D": w_down[0],
        }
    )

    def transfer(at, name, work, read):
        r.add(at, name, work, read, due=at + HOLD)
        return at + HOLD + 1

    ready, pieces = {}, {}
    for a in "tc":
        ready[a] = 0
        for k in range(count):
            if k < count - 1:
                transfer(START[a][k], (a, k + 1), over_z, (a, k))
            work, read = {
                "x": (over_x, (a + "y", k)),
                "y": (over_y, (a + "x", k)),
                "z": (over_z, (a + "d", k - 1)),
            }[ROUTE[a][k]]
            ready[a] = max(
                ready[a],
                transfer(START[a + "x"][k], (a + "x", k), over_x, (a, k)),
                transfer(START[a + "y"][k], (a + "y", k), over_y, (a, k)),
                transfer(START[a + "d"][k], (a + "d", k), work, read),
            )
        pieces[a] = [(a + which, k) if which else (a, k) for k in range(count) for which in ("", "x", "y", "d")]
    m_at, m_terms, g_at, g_terms = KERNELS

    cores = [[i, i + 1] for i in range(0, experts, 2)]
    for name, due in zip("GUD", PAIRED, strict=True):
        r.add(0, name + "s", lambda w: lax.all_gather(w, "expert", axis_index_groups=cores), name, due=due)
    wides, talls = ("G", "U", "Gs", "Us"), ("D", "Ds")
    for name, work in zip(("wx", "wy", "wd"), (over_x, over_y, over_xy), strict=True):
        r.add(0, name, work, "w")

    def share_pair(*blocks):
        share = below(*blocks)
        return beside(*[lax.dynamic_slice_in_dim(share, me ^ i, 1, 1) for i in range(2)])

    r.add(6, "s", share_pair, "w", "wx", "wy", "wd")

    def sizes(dtype, *columns):
        return [jax.ShapeDtypeStruct((4 * rows, n), dtype) for n in columns]

    def activations(total, extras, outs):
        share, both, weighted = extras[0][...], *outs
        both[...] = total[...]
        for i in range(2):
            gate = total[:, 2 * i * units : (2 * i + 1) * units]
            up = total[:, (2 * i + 1) * units : (2 * i + 2) * units]
            value = share[:, i : i + 1] * (gate * jax.nn.sigmoid(gate) * up)
            weighted[:, i * units : (i + 1) * units] = as_bf16(value)

    def gradients(total, extras, outs):
        share, both = extras[0][...], extras[1]
        to_tokens, to_weights, inner = outs
        for i in range(2):
            gate = both[:, 2 * i * units : (2 * i + 1) * units]
            up = both[:, (2 * i + 1) * units : (2 * i + 2) * units]
            d_plain = total[:, i * units : (i + 1) * units]
            weight = share[:, i : i + 1]
            sigmoid_gate = jax.nn.sigmoid(gate)
            silu_gate = gate * sigmoid_gate
            inner[:, i : i + 1] = jnp.sum(silu_gate * up * d_plain, axis=1, keepdims=True)
            d_hidden = weight * d_plain
            d_gate = d_hidden * up * sigmoid_gate * (1.0 + gate * (1.0 - sigmoid_gate))
            d_up = d_hidden * silu_gate
            to_weights[:, 2 * i * units : (2 * i + 1) * units] = as_bf16(d_gate)
            to_weights[:, (2 * i + 1) * units : (2 * i + 2) * units] = as_bf16(d_up)
            to_tokens[:, 2 * i * units : (2 * i + 1) * units] = as_bf16(weight * d_gate)
            to_tokens[:, (2 * i + 1) * units : (2 * i + 2) * units] = as_bf16(weight * d_up)

    def steps_of(values):
        return [values[4 * k : 4 * k + 4] for k in range(count)]

    def forward(share, *values):
        outs = sizes(jnp.float32, 4 * units) + sizes(jnp.bfloat16, 2 * units)
        parts, weights = steps_of(values), values[4 * count :]
        return summed_product(parts, weights, 0, place_at, [share], activations, outs)

    def backward(share, both, *values):
        outs = sizes(jnp.bfloat16, 4 * units, 4 * units) + sizes(jnp.float32, 2)
        parts, weights = steps_of(values), values[4 * count :]
        return summed_product(parts, weights, 1, place_at, [share, both], gradients, outs)

    def unpacked(at, name, work, names, *reads):
        r.add(at, name, work, *reads)
        for i, part in enumerate(names):
            r.add(at, part, lambda v, i=i: v[i], name)

    unpacked(m_at, "H", forward, ("h", "v"), "s", *pieces["t"], *wides)
    unpacked(g_at, "E", backward, ("g", "b", "i"), "s", "h", *pieces["c"], *talls)

    own, side, front, far = range(4)
    layout = {
        "x0": [(0, side)],
        "y0": [(0, front)],
        "x1": [(1, side), (2, side)],
        "y1": [(1, front), (3, front), (3, far)],
        "f0": [(0, far)],
        "f1": [(1, far)],
        "f2": [(2, far)],
        "x3": [(3, side)],
        "y2": [(2, front)],
    }
    layout |= {k: [(k, own)] for k in range(count)}

    def cut(value, n):
        return value[n * rows : (n + 1) * rows]

    def add_up(*terms):
        return as_bf16(sum([as_f32(v) for v in terms[1:]], as_f32(terms[0])))

    for o, at, left, weights, axis in (("m", m_terms, "v", talls, 1), ("g", g_terms, "g", wides, 0)):

        def work(left, *weights, axis=axis):
            return block_terms(left, weights, axis, place_at, count, list(layout.values()), 4)

        unpacked(at, o + "P", work, [(o + "p", name) for name in layout], left, *weights)

        def send(name, work, terms, *reads, o=o):
            start, due = SUMS[o + name]
            r.add(start, (o + "s", name), terms, (o + "p", name), *[(o, n) for n in reads])
            r.add(start, (o, name), work, (o + "s", name), due=due)

        for name, work in (("x0", over_x), ("y0", over_y), ("f0", over_z), ("x1", over_x), ("y1", over_y)):
            send(name, work, lambda v: v)
        send("f1", over_z, add_up, "f0")
        send("f2", over_x, add_up, "f1")
        send("y2", over_y, add_up, "f2")
        send("x3", over_x, lambda v, y: add_up(v, cut(y, 2)), "y1")

        def send_own(k, terms, *reads, o=o):
            start, due = SUMS[o + "z"][k]
            add = closing_sum if (o, k) == ("g", 3) else add_up
            r.add(start, (o + "s", k), lambda *v: add(*terms(*v)), (o + "p", k), *[(o, n) for n in reads])
            if k < count - 1:
                r.add(start, (o, k), over_z, (o + "s", k), due=due)

        send_own(0, lambda v, x, y: (v, x, y), "x0", "y0")
        send_own(1, lambda v, x, y, z: (v, cut(x, 0), cut(y, 0), z), "x1", "y1", 0)
        send_own(2, lambda v, x, y, z: (v, cut(x, 1), y, z), "x1", "y2", 1)
        send_own(3, lambda v, x, y, z: (v, x, cut(y, 1), z), "x3", "y1", 2)

    for q, work in enumerate((over_x, over_y, over_xy), 1):
        r.add(INNER[0], ("n", q), lambda v, work=work, q=q: work(v[q * rows : (q + 1) * rows]), "i")

    def route_sums(inner, *others):
        total = 0.0
        first = jnp.where(me % 2 == 1, 4, 2)
        for bits, found in zip((0, first, 6 - first, 6), (inner[:rows], *others), strict=True):
            for i in range(2):
                total += jnp.where(route_ids == me ^ bits ^ i, found[:, i : i + 1], 0.0)
        return total

    r.add(INNER[0] + 1, ("o", 0), route_sums, "i", *[("n", q) for q in (1, 2, 3)])
    for k in range(1, count):
        r.add(INNER[1], ("o", k), along_z(k), ("o", 0))

    def in_order(*turns):
        turns = jnp.stack(turns)
        return sum(lax.dynamic_index_in_dim(turns, part_of(k), 0, False) for k in range(count))

    r.add(INNER[1] + 1, "o", in_order, *[("o", k) for k in range(count)])

    def tall_terms(left, *parts):
        return weight_grads(steps_of(parts), left, place_at, 1, True)

    def wide_terms(left, *parts):
        return weight_grads(steps_of(parts), left, place_at, 2, False)

    def summed(*terms):
        return [
            lax.psum_scatter(v, "expert", scatter_dimension=0, axis_index_groups=cores) for v in terms
        ]

    end = max(step[1] for step in r.steps)
    unpacked(GRADS[0], "A", tall_terms, ["A0", "A1"], "v", *pieces["c"])
    r.add(GRADS[0] + 1, "Ax", over_core, "A1", due=GRADS[0] + 3)
    r.add(GRADS[0] + 4, "AA", add_up, "A0", "Ax")
    unpacked(GRADS[1], "B", wide_terms, ["B0", "B1"], "b", *pieces["t"])
    r.add(GRADS[1] + 1, "BB", summed, "B0", "B1", due=end)
    mixed, grad_tokens, grad_route, wide, tall = r.run([("ms", count - 1), ("gs", count - 1), "o", "BB", "AA"])
    return mixed, grad_tokens, grad_route, wide[0][None], wide[1][None], tall[None]


def local(tokens, route_ids, route_weights, cotangent, w_gate, w_up, w_down):
    experts = lax.axis_size("expert")
    capacity = 4 * tokens.shape[0] // experts
    whole = 2 * capacity >= tokens.shape[0] and (experts, lax.axis_size("tensor")) == (8, 4)
    plan = chip_plan if whole else slot_plan
    return plan(tokens, route_ids, route_weights, cotangent, w_gate, w_up, w_down)


def solution(mesh):
    placed = (
        P("expert", "tensor"),
        P("expert", None),
        P("expert", None),
        P("expert", "tensor"),
        P("expert", None, "tensor"),
        P("expert", None, "tensor"),
        P("expert", "tensor", None),
    )
    return jax.shard_map(
        local,
        mesh=mesh,
        in_specs=placed,
        out_specs=(
            P("expert", "tensor"),
            P("expert", "tensor"),
            P("expert", None),
            P("expert", None, "tensor"),
            P("expert", None, "tensor"),
            P("expert", "tensor", None),
        ),
        check_vma=False,
    )
```
